768 devices in a mesh: dom: 96 (over z, y), sub: 8 (over x, core).
Axes of the slice: x: 4, y: 8, z: 12, core: 2. Of those that a mesh axis runs over, the one named last changes fastest.
Arguments:
- feats: bfloat16 [768, 393216], P('sub', 'dom'), may hold values from -6 to 6
- weight: bfloat16 [768, 768], replicated, may hold values from -0.21875 to 0.21875
- edge_dst: int32 [96, 64], P('dom'), may hold values from 0 to 31
- edge_src: int32 [96, 64], P('dom'), may hold values from 0 to 47, as said below
- edge_mask: int32 [96, 64, 128, 128], P('dom'), may hold values from 0 to 1
- send_list: int32 [96, 4, 4], P('dom'), may hold values from 0 to 31
- send_count: int32 [96, 4], P('dom'), may hold values from 1 to 4, as said below
- cotangent: bfloat16 [768, 393216], P(None, ('dom', 'sub')), may hold values from -6 to 6
Outputs:
- hidden: bfloat16 [768, 393216], P(None, ('dom', 'sub'))
- d_feats: bfloat16 [768, 393216], P('sub', 'dom')
- d_weight: float32 [768, 768], replicated
The draws below stay inside these ranges and needn't reach their ends.
Inputs may be any that keep to these rules, and one draw needn't show every extreme that they name: `edge_src`: A tile 32 + j * 4 + k of partition p is read only where k < send_count[(p - r_j) mod 96, j]. Slots from send_count on are padding.
All inputs are finite; a program needn't handle non-finite values.
Results may differ from the reference program's by a relative error of at most 0.0068.
Values may be sent and summed in bfloat16 or wider, within the bound.
A program may use at most 64 MiB of HBM per device.

```python
import jax
import jax.numpy as jnp
from jax import lax

D = 768
BLOCK = 128
NB = 32
OFFS = 4
CAP = 4
EDGES = 64
TABLE = 48
PARTITIONS = 96
LABELS = 393216


def cycle_counts(key):
    key = jax.random.fold_in(key, 11)
    first, second = jax.random.split(key)
    rotation = jax.random.randint(first, (), 0, 3)
    counted = jax.random.randint(second, (PARTITIONS, OFFS), 1, CAP + 1)
    part_ids = jnp.arange(PARTITIONS, dtype=jnp.int32)[:, None]
    offset_ids = jnp.arange(OFFS, dtype=jnp.int32)[None, :]
    return jnp.where((part_ids + offset_ids + rotation) % 3 == 0, CAP, counted).astype(jnp.int32)


def draw_send_count(key, part):
    return cycle_counts(key)


def draw_edge_src(key, part):
    counts = cycle_counts(key)
    key = jax.random.fold_in(key, 3)
    k_offset, k_remote, k_slot, k_local = jax.random.split(key, 4)
    edge_ids = jnp.arange(EDGES, dtype=jnp.int32)[None, :]
    part_ids = jnp.arange(PARTITIONS, dtype=jnp.int32)[:, None]
    picked = jax.random.randint(k_offset, (PARTITIONS, EDGES), 0, OFFS)
    offsets = jnp.where(edge_ids < OFFS, edge_ids, jnp.where(edge_ids == OFFS, OFFS - 1, picked))
    remote = (edge_ids <= OFFS) | (jax.random.randint(k_remote, (PARTITIONS, EDGES), 0, 2) == 1)
    distance = (offsets // 2 + 1) * (1 - 2 * (offsets % 2))
    sender = (part_ids - distance) % PARTITIONS
    live_count = counts[sender, offsets]
    slot = jnp.where(edge_ids == OFFS, live_count - 1, jax.random.randint(k_slot, (PARTITIONS, EDGES), 0, CAP) % live_count)
    local = jax.random.randint(k_local, (PARTITIONS, EDGES), 0, NB)
    return jnp.where(remote, NB + offsets * CAP + slot, local).astype(jnp.int32)


def draw_edge_mask(key, part):
    key = jax.random.fold_in(key, 5)
    k_rate, k_bits = jax.random.split(key)
    rates = jax.random.randint(k_rate, (PARTITIONS, EDGES, 1, 1), 30, 300)
    draws = jax.random.randint(k_bits, (PARTITIONS, EDGES, BLOCK, BLOCK), 0, 1000)
    return (draws < rates).astype(jnp.int32)


def touch_ends(drawn, rng, smallest, top_value):
    shape = drawn.shape
    spot = [jax.random.randint(jax.random.fold_in(rng, axis), (), 0, shape[axis]) for axis in range(len(shape))]
    drawn = drawn.at[tuple(spot)].set(smallest)
    longest = shape.index(max(shape))
    spot[longest] = (spot[longest] + 1) % shape[longest]
    return drawn.at[tuple(spot)].set(top_value)


def shard_levels(rng, extent, cuts, least, top_value):
    def one(axis_at, blocks):
        heights = jax.random.uniform(jax.random.fold_in(jax.random.fold_in(rng, 6), axis_at), (blocks,), jnp.float32, least / len(cuts), top_value / len(cuts))
        return jnp.repeat(jnp.exp(heights), extent[axis_at] // blocks).reshape((-1,) + (1,) * (len(extent) - axis_at - 1))

    gain = one(*cuts[0])
    for cut in cuts[1:]:
        gain = gain * one(*cut)
    return gain


def noise(key, dims, scale, limit, shards=(), kind=jnp.bfloat16):
    result = scale * jax.random.normal(key, dims, jnp.float32)
    if shards:
        result = result * shard_levels(key, dims, shards, -0.22, 0.18)
    return jnp.clip(result, -limit, limit).astype(kind)


def setup_inputs(seed: int = 0) -> dict:
    streams_of = jax.random.split(jax.random.key(seed), 9)
    return {
        "feats": noise(streams_of[0], (D, LABELS), 1.0, 6.0, ((0, 8), (1, 96))),
        "weight": noise(streams_of[1], (D, D), D ** -0.5, 0.21875),
        "edge_dst": touch_ends(jax.random.randint(streams_of[2], (PARTITIONS, EDGES), 0, NB), jax.random.fold_in(streams_of[2], 1), 0, NB - 1).astype(jnp.int32),
        "edge_src": draw_edge_src(jax.random.fold_in(streams_of[8], 71), 0),
        "edge_mask": draw_edge_mask(jax.random.fold_in(streams_of[8], 71), 0),
        "send_list": touch_ends(jax.random.randint(streams_of[5], (PARTITIONS, OFFS, CAP), 0, NB), jax.random.fold_in(streams_of[5], 1), 0, NB - 1).astype(jnp.int32),
        "send_count": draw_send_count(jax.random.fold_in(streams_of[8], 71), 0),
        "cotangent": noise(streams_of[7], (D, LABELS), 1.0, 6.0, ((1, 768),)),
    }


def offset_of(position):
    return (position // 2 + 1) * (1 - 2 * (position % 2))

def reference(feats, weight, edge_dst, edge_src, edge_mask, send_list, send_count, cotangent):
    highest = lax.Precision.HIGHEST
    partitions = edge_dst.shape[0]
    label_span = NB * BLOCK
    all_tiles = feats.reshape(D, partitions, NB, BLOCK)
    cot_blocks = cotangent.reshape(D, partitions, label_span)
    slot_index = jnp.arange(CAP, dtype=jnp.int32)

    def forward_backward(weight_grad, part_id):
        own_tiles = lax.dynamic_index_in_dim(all_tiles, part_id, 1, False)
        pieces = [own_tiles]
        for position in range(OFFS):
            sender = (part_id - offset_of(position)) % partitions
            sender_tiles = lax.dynamic_index_in_dim(all_tiles, sender, 1, False)
            chosen = jnp.take(sender_tiles, send_list[sender, position], axis=1)
            slot_live = slot_index < send_count[sender, position]
            pieces.append(jnp.where(slot_live[None, :, None], chosen, jnp.zeros_like(chosen)))
        source_table = jnp.concatenate(pieces, axis=1)
        targets = edge_dst[part_id]
        sources = edge_src[part_id]
        tile_masks = edge_mask[part_id].astype(jnp.float32)
        gathered = jnp.take(source_table, sources, axis=1).astype(jnp.float32)
        products = jnp.einsum('deq,epq->edp', gathered, tile_masks, precision=highest)
        summed = jax.ops.segment_sum(products, targets, num_segments=NB)
        degree = jax.ops.segment_sum(lax.optimization_barrier(jnp.sum(tile_masks, axis=2)), targets, num_segments=NB)
        row_scale = lax.rsqrt(1.0 + degree)
        aggregated = ((own_tiles.astype(jnp.float32) + jnp.transpose(summed, (1, 0, 2))) * row_scale[None]).astype(jnp.bfloat16)
        agg_flat = aggregated.reshape(D, label_span)
        pre_act = jnp.dot(weight, agg_flat, preferred_element_type=jnp.float32)
        hidden = jax.nn.silu(pre_act).astype(jnp.bfloat16)
        sigmoid_pre = jax.nn.sigmoid(pre_act)
        cot_block = lax.dynamic_index_in_dim(cot_blocks, part_id, 1, False).astype(jnp.float32)
        d_pre = (cot_block * sigmoid_pre * (1.0 + pre_act * (1.0 - sigmoid_pre))).astype(jnp.bfloat16)
        part_term = jnp.dot(d_pre, agg_flat.T, preferred_element_type=jnp.float32)
        d_agg = jnp.dot(weight.T, d_pre, preferred_element_type=jnp.float32).astype(jnp.bfloat16)
        scaled = (d_agg.reshape(D, NB, BLOCK).astype(jnp.float32) * row_scale[None]).astype(jnp.bfloat16)
        by_edge = jnp.take(scaled, targets, axis=1).astype(jnp.float32)
        d_source = jnp.einsum('dep,epq->edq', by_edge, tile_masks, precision=highest)
        d_table = jax.ops.segment_sum(d_source, sources, num_segments=TABLE)
        local_total = scaled.astype(jnp.float32) + jnp.transpose(d_table[:NB], (1, 0, 2))
        remote_grads = d_table[NB:].reshape(OFFS, CAP, D, BLOCK).astype(jnp.bfloat16)
        return (weight_grad + part_term, (hidden, local_total, remote_grads))
    part_ids = jnp.arange(partitions, dtype=jnp.int32)
    d_weight, (hiddens, local_totals, remotes) = lax.scan(forward_backward, jnp.zeros((D, D), jnp.float32), part_ids)

    def collect(part_id):
        running = local_totals[part_id]
        for position in range(OFFS):
            receiver = (part_id + offset_of(position)) % partitions
            grad_piece = remotes[receiver, position].astype(jnp.float32)
            slot_live = (slot_index < send_count[part_id, position]).astype(jnp.float32)
            send_hot = jax.nn.one_hot(send_list[part_id, position], NB, dtype=jnp.float32) * slot_live[:, None]
            running = running + jnp.einsum('kdq,kb->dbq', grad_piece, send_hot, precision=highest)
        return running.astype(jnp.bfloat16)
    d_parts = lax.map(collect, part_ids)
    hidden_out = jnp.transpose(hiddens, (1, 0, 2)).reshape(D, partitions * label_span)
    d_feats = jnp.transpose(d_parts, (1, 0, 2, 3)).reshape(D, partitions * label_span)
    return (hidden_out, d_feats, d_weight)
```

```python
import functools

import jax
import jax.numpy as jnp
from jax import lax
from jax.experimental import pallas as pl
from jax.experimental.pallas import tpu as pltpu
from jax.sharding import PartitionSpec as P

ROWS_Y = 8
CORES = 2
ONES = 16
F32 = jnp.float32
BF16 = jnp.bfloat16
FAR_FIRST = {4: (2, 1, 3, 0), 2: (1, 0)}


def offset_of(position):
    return (position // 2 + 1) * (1 - 2 * (position % 2))


def order_by(keys, attributes, key_count):
    size = keys.shape[1]
    row = lax.broadcasted_iota(jnp.int32, (size, size), 0)
    lane = lax.broadcasted_iota(jnp.int32, (size, size), 1)

    def column(values):
        spread = jnp.broadcast_to(values, (size, size))
        return jnp.sum(jnp.where(row == lane, spread, 0.0), axis=1, keepdims=True)

    keys_column = column(keys)
    same = jnp.broadcast_to(keys, (size, size)) == keys_column
    less = jnp.broadcast_to(keys, (size, size)) < keys_column
    earlier = same & (lane < row)
    rank = jnp.sum(jnp.where(less | earlier, 1.0, 0.0), axis=1, keepdims=True)
    keep = jnp.minimum(jnp.sum(jnp.where(earlier, 1.0, 0.0), axis=1, keepdims=True), 1.0)
    hit = jnp.where(rank == lane.astype(F32), 1.0, 0.0)

    def placed(values):
        return jnp.sum(hit * values, axis=0, keepdims=True)

    wanted = lax.broadcasted_iota(jnp.int32, (size, key_count), 1).astype(F32)
    last = jnp.sum(jnp.where(keys_column <= wanted, 1.0, 0.0), axis=0, keepdims=True) - 1.0
    present = jnp.sum(jnp.where(keys_column == wanted, 1.0, 0.0), axis=0, keepdims=True)
    index_column = lax.broadcasted_iota(jnp.int32, (size, 1), 0).astype(F32)
    return (
        [placed(index_column)]
        + [placed(column(values)) for values in attributes]
        + [placed(keep), jnp.maximum(last, 0.0), jnp.minimum(present, 1.0)]
    )


def plan_kernel(blocks, table_len, list_ref, count_ref, dst_ref, src_ref, out_ref):
    _, offsets, capacity = list_ref.shape
    slots = offsets * capacity
    dst = dst_ref[...].astype(F32)
    src = src_ref[...].astype(F32)
    lane = lax.broadcasted_iota(jnp.int32, (1, slots), 1)
    listed = jnp.zeros((1, slots), jnp.int32)
    live = jnp.zeros((1, slots), jnp.int32)
    for j in range(offsets):
        for k in range(capacity):
            here = lane == j * capacity + k
            listed = jnp.where(here, list_ref[0, j, k], listed)
            live = jnp.where(here & (k < count_ref[0, j]), 1, live)
    owner = jnp.where(live == 1, listed, blocks).astype(F32)
    rows = (
        order_by(dst, [src], blocks)
        + order_by(src, [dst], table_len)
        + [listed.astype(F32)]
        + order_by(owner, [], blocks)
    )
    out_ref[...] = jnp.zeros_like(out_ref)
    for index, values in enumerate(rows):
        out_ref[index : index + 1, : values.shape[1]] = values.astype(jnp.int32)


def kernel(
    cols_x,
    plan,
    feats,
    weight,
    mask,
    cot,
    hidden,
    d_feats,
    d_weight,
    table,
    mask_int,
    mask_half,
    sums,
    w,
    wt,
    cot_v,
    outgoing,
    incoming,
    agg,
    full,
    scales,
    hid,
    d_pre,
    d_agg,
    dw_out,
    dw_own,
    core_in,
    x_out,
    x_in,
    z_out,
    z_in,
    y_all,
    gathered,
    back,
    scaled,
    returning,
    returned,
    slot_sums,
    result,
    local_sem,
    tile_sem,
    perm_sem,
    ret_sem,
    a2a_sem,
    back_sem,
    core_sem,
    x_sem,
    z_sem,
    y_sem,
    gz_sem,
    gx_sem,
    gc_sem,
):
    width, span = feats.shape
    edges, block, _ = mask.shape
    features = weight.shape[0]
    blocks = span // block
    slots = returned.shape[0]
    offsets = perm_sem.shape[1]
    capacity = slots // offsets
    subs = cols_x * CORES
    per_sub = blocks // subs
    half = features // CORES
    xrows = half // cols_x
    doms = lax.axis_size("dom")
    deep = doms // ROWS_Y
    wide = features // 2

    dom, sub = lax.axis_index("dom"), lax.axis_index("sub")
    z, y = dom // ROWS_Y, dom % ROWS_Y
    x, core = sub // CORES, sub % CORES
    sibling = x * CORES + 1 - core

    def tile(index):
        return pl.ds(pl.multiple_of(index * block, block), block)

    def push(src, dst, sems, index, to_dom, to_sub):
        copy = pltpu.make_async_remote_copy(
            src_ref=src,
            dst_ref=dst,
            send_sem=sems.at[0, index],
            recv_sem=sems.at[1, index],
            device_id=(to_dom, to_sub),
            device_id_type=pl.DeviceIdType.MESH,
        )
        copy.start()
        return copy

    def fetch(src, dst, index):
        copy = pltpu.make_async_copy(src, dst, local_sem.at[index])
        copy.start()
        return copy

    in_dom = [lax.rem(dom + offset_of(j) + doms, doms) for j in range(offsets)]
    against = [lax.rem(dom - offset_of(j) + doms, doms) for j in range(offsets)]
    in_sub = [
        (o * CORES + d, lax.rem(x + o, cols_x) * CORES + lax.rem(core + d, CORES))
        for o in FAR_FIRST[cols_x]
        for d in range(CORES)
        if o or d
    ]
    in_x = [(o, lax.rem(x + o, cols_x)) for o in FAR_FIRST[cols_x] if o]
    in_z = [(o, lax.rem(z + o, deep)) for o in range(1, deep)]
    in_y = [(o, lax.rem(y + o, ROWS_Y)) for o in range(1, ROWS_Y)]

    barrier = pltpu.get_barrier_semaphore()
    partners = (
        [(d, sub) for d in in_dom]
        + [(dom, s) for _, s in in_sub]
        + [(other * ROWS_Y + y, sub) for _, other in in_z]
        + [(z * ROWS_Y + other, sub) for _, other in in_y]
    )
    for partner in partners:
        pl.semaphore_signal(
            barrier, inc=1, device_id=partner, device_id_type=pl.DeviceIdType.MESH
        )

    def own_tile(b):
        return pltpu.make_async_copy(feats.at[:, tile(b)], table.at[b, :width], tile_sem.at[b])

    def start_tile(b, carry):
        own_tile(b).start()
        return carry

    lax.fori_loop(0, blocks, start_tile, 0)
    quarter = edges // 4
    mask_in = [
        fetch(mask.at[pl.ds(i * quarter, quarter)], mask_int.at[pl.ds(i * quarter, quarter)], 1 + i)
        for i in range(4)
    ]
    w_in = fetch(weight, w, 5)
    cot_in = fetch(cot, cot_v, 6)

    def ones_below(t, carry):
        table[t, width:, :] = jnp.ones((ONES, block), BF16)
        return carry

    lax.fori_loop(0, blocks + slots, ones_below, 0)

    def wait_tile(b, carry):
        own_tile(b).wait()
        return carry

    lax.fori_loop(0, blocks, wait_tile, 0)
    for slot in range(slots):
        outgoing[slot] = table[plan[10, slot]][:width]
    pl.semaphore_wait(barrier, len(partners))

    sent = [
        push(
            outgoing.at[pl.ds(j * capacity, capacity)],
            incoming.at[pl.ds(j * capacity, capacity)],
            perm_sem,
            j,
            in_dom[j],
            sub,
        )
        for j in range(offsets)
    ]
    for i in range(4):
        mask_in[i].wait()

        def halve(e, carry):
            mask_half[e] = mask_int[e].astype(F32).astype(BF16)
            return carry

        lax.fori_loop(i * quarter, (i + 1) * quarter, halve, 0, unroll=2)
    w_in.wait()
    strip = features // 4
    for i in range(4):
        wt[:, i * strip : (i + 1) * strip] = w[i * strip : (i + 1) * strip, :].T
    for copy in sent:
        copy.wait_recv()
    table[blocks:, :width, :] = incoming[...]

    def forward(q, running):
        product = lax.dot_general(
            table[plan[1, q]],
            mask_half[plan[0, q]],
            (((1,), (1,)), ((), ())),
            preferred_element_type=F32,
        )
        running = running * plan[2, q].astype(F32) + product
        sums[q] = running
        return running

    lax.fori_loop(0, edges, forward, jnp.zeros((width + ONES, block), F32), unroll=4)

    def aggregate(s):
        def one(i, carry):
            b = s * per_sub + i
            total = sums[plan[3, b]] * plan[4, b].astype(F32)
            scale = lax.rsqrt(1.0 + total[width : width + 1])
            scales[b] = jnp.broadcast_to(scale, (8, block))
            own = table[b, :width, :].astype(F32)
            agg[s, :, tile(i)] = ((own + total[:width]) * scale).astype(BF16)
            return carry

        lax.fori_loop(0, per_sub, one, 0)

    own_rows = pl.ds(pl.multiple_of(sub * width, width), width)
    across = []
    for index, s in in_sub:
        aggregate(s)
        across.append(push(agg.at[s], full.at[own_rows], a2a_sem, index, dom, s))
    aggregate(sub)
    full[own_rows, :] = agg[sub]
    cot_in.wait()
    for copy in across:
        copy.wait_recv()

    def transform(i, carry):
        rows = pl.ds(pl.multiple_of(i * strip, strip), strip)
        pre = jnp.dot(w[rows, :], full[...], preferred_element_type=F32)
        gate = 1.0 / (1.0 + jnp.exp(-pre))
        hid[rows, :] = (pre * gate).astype(BF16)
        d_pre[rows, :] = (
            cot_v[rows, :].astype(F32) * gate * (1.0 + pre * (1.0 - gate))
        ).astype(BF16)
        return carry

    lax.fori_loop(0, 4, transform, 0)
    hid_out = fetch(hid, hidden, 7)

    def term(i):
        rows = pl.ds(pl.multiple_of(i * strip, strip), strip)
        return lax.dot_general(
            d_pre[rows, :], full[...], (((1,), (1,)), ((), ())), preferred_element_type=F32
        )

    def local_rows(i):
        return pl.ds(pl.multiple_of(i * strip, strip), strip)

    def for_sibling(i, carry):
        dw_out[local_rows(i), :] = term((1 - core) * 2 + i).astype(BF16)
        return carry

    lax.fori_loop(0, 2, for_sibling, 0)
    to_core = push(dw_out, core_in, core_sem, 0, dom, sibling)

    def for_self(i, carry):
        dw_own[local_rows(i), :] = term(core * 2 + i)
        return carry

    lax.fori_loop(0, 2, for_self, 0)
    pair = CORES * width

    def gradient(i, carry):
        rows = pl.ds(pl.multiple_of(i * pair, pair), pair)
        product = jnp.dot(wt[rows, :], d_pre[...], preferred_element_type=F32).astype(BF16)
        for k in range(per_sub):
            d_agg[k, rows, :] = product[:, k * block : (k + 1) * block]
        return carry

    lax.fori_loop(0, cols_x, gradient, 0)

    def x_rows(i):
        return pl.ds(pl.multiple_of(i * xrows, xrows), xrows)

    to_core.wait_recv()

    def add_core(i, carry):
        total = dw_own[x_rows(i), :] + core_in[x_rows(i), :].astype(F32)
        dw_own[x_rows(i), :] = total
        x_out[x_rows(i), :] = total.astype(BF16)
        return carry

    lax.fori_loop(0, cols_x, add_core, 0)
    to_x = [
        push(x_out.at[x_rows(other)], x_in.at[o - 1], x_sem, o, dom, other * CORES + core)
        for o, other in in_x
    ]
    own_blocks = pl.ds(sub * per_sub, per_sub)
    backward = [
        push(
            d_agg.at[:, pl.ds(pl.multiple_of(s * width, width), width)],
            back.at[own_blocks],
            back_sem,
            index,
            dom,
            s,
        )
        for index, s in in_sub
    ]
    back[own_blocks] = d_agg[:, own_rows, :]

    def z_part(i):
        return (
            pl.ds(pl.multiple_of((i // 2) * 16, 16), 16),
            pl.ds(pl.multiple_of((i % 2) * wide, wide), wide),
        )

    for copy in to_x:
        copy.wait_recv()
    total = dw_own[x_rows(x), :]
    for o in range(cols_x - 1):
        total = total + x_in[o].astype(F32)
    dw_own[:xrows, :] = total
    z_out[...] = total.astype(BF16)
    to_z = [
        push(z_out.at[z_part(other)], z_in.at[o - 1], z_sem, o, other * ROWS_Y + y, sub)
        for o, other in in_z
    ]
    for copy in backward:
        copy.wait_recv()

    def rescale(b, carry):
        scaled[b] = (back[b].astype(F32) * scales[b][:1]).astype(BF16)
        return carry

    lax.fori_loop(0, blocks, rescale, 0, unroll=2)
    for copy in to_z:
        copy.wait_recv()
    rows, columns = z_part(z)
    total = dw_own[rows, columns]
    for o in range(deep - 1):
        total = total + z_in[o].astype(F32)
    y_all[y] = total.astype(BF16)
    to_y = [
        push(y_all.at[y], y_all.at[y], y_sem, o, z * ROWS_Y + other, sub) for o, other in in_y
    ]

    def backward_edge(q, running):
        product = jnp.dot(
            scaled[plan[6, q]], mask_half[plan[5, q]], preferred_element_type=F32
        )
        running = running * plan[7, q].astype(F32) + product
        sums[q, :width, :] = running
        return running

    lax.fori_loop(0, edges, backward_edge, jnp.zeros((width, block), F32), unroll=4)
    home = []
    for j in range(offsets):
        for k in range(capacity):
            t = blocks + j * capacity + k
            returning[j * capacity + k] = (
                sums[plan[8, t]][:width] * plan[9, t].astype(F32)
            ).astype(BF16)
        home.append(
            push(
                returning.at[pl.ds(j * capacity, capacity)],
                returned.at[pl.ds(j * capacity, capacity)],
                ret_sem,
                j,
                against[j],
                sub,
            )
        )
    for copy in to_y:
        copy.wait_recv()
    for copy in to_y:
        copy.wait_send()
    total = y_all[0].astype(F32)
    for other in range(1, ROWS_Y):
        total = total + y_all[other].astype(F32)

    def x_strip(of_core, of_x):
        return pl.ds(pl.multiple_of(of_core * half + of_x * xrows, xrows), xrows)

    mine = (
        pl.ds(pl.multiple_of(core * half + x * xrows + (z // 2) * 16, 16), 16),
        pl.ds(pl.multiple_of((z % 2) * wide, wide), wide),
    )
    gathered[mine] = total.astype(BF16)
    over_z = [
        push(gathered.at[mine], gathered.at[mine], gz_sem, o, other * ROWS_Y + y, sub)
        for o, other in in_z
    ]
    for copy in over_z:
        copy.wait_recv()
    strip_x = gathered.at[x_strip(core, x)]
    over_x = [
        push(strip_x, strip_x, gx_sem, o, dom, other * CORES + core) for o, other in in_x
    ]
    over_core = [push(strip_x, strip_x, gc_sem, 0, dom, sibling)]
    for copy in home:
        copy.wait_recv()

    def add_slot(i, running):
        running = running * plan[12, i].astype(F32) + returned[plan[11, i]].astype(F32)
        slot_sums[i] = running
        return running

    lax.fori_loop(0, slots, add_slot, jnp.zeros((width, block), F32))

    def finish(b, carry):
        result[:, tile(b)] = (
            scaled[b].astype(F32)
            + sums[plan[8, b]][:width] * plan[9, b].astype(F32)
            + slot_sums[plan[13, b]] * plan[14, b].astype(F32)
        ).astype(BF16)
        return carry

    lax.fori_loop(0, blocks, finish, 0, unroll=2)
    d_feats_out = fetch(result, d_feats, 8)
    for (o, _), copy in zip(in_x, over_x):
        copy.wait_recv()
        arrived = gathered.at[x_strip(core, lax.rem(x - o + cols_x, cols_x))]
        over_core.append(push(arrived, arrived, gc_sem, o, dom, sibling))
    for copy in over_core:
        copy.wait_recv()
    d_weight_out = fetch(gathered, d_weight, 9)
    for copy in (
        sent + across + [to_core] + to_x + backward + to_z + home + over_z + over_x + over_core
    ):
        copy.wait_send()
    hid_out.wait()
    d_feats_out.wait()
    d_weight_out.wait()


def shards(cols_x, feats, weight, edge_dst, edge_src, edge_mask, send_list, send_count, cotangent):
    width, span = feats.shape
    _, edges, block, _ = edge_mask.shape
    features = weight.shape[0]
    blocks = span // block
    _, offsets, capacity = send_list.shape
    slots = offsets * capacity
    table_len = blocks + slots
    subs = cols_x * CORES
    labels = span // subs
    half = features // CORES
    xrows = half // cols_x
    deep = lax.axis_size("dom") // ROWS_Y
    vmem, smem, anywhere = (
        pl.BlockSpec(memory_space=space) for space in (pltpu.VMEM, pltpu.SMEM, pl.ANY)
    )
    plan = pl.pallas_call(
        functools.partial(plan_kernel, blocks, table_len),
        out_shape=jax.ShapeDtypeStruct((16, 128), jnp.int32),
        in_specs=[smem, smem, vmem, vmem],
        out_specs=vmem,
    )(send_list, send_count, edge_dst, edge_src)
    dma = pltpu.SemaphoreType.DMA
    hidden, d_feats, d_weight = pl.pallas_call(
        functools.partial(kernel, cols_x),
        out_shape=(
            jax.ShapeDtypeStruct((features, labels), BF16),
            jax.ShapeDtypeStruct((width, span), BF16),
            jax.ShapeDtypeStruct((features, features), BF16),
        ),
        in_specs=[smem] + [anywhere] * 4,
        out_specs=(anywhere,) * 3,
        scratch_shapes=[
            pltpu.VMEM((table_len, width + ONES, block), BF16),
            pltpu.VMEM((edges, block, block), jnp.int32),
            pltpu.VMEM((edges, block, block), BF16),
            pltpu.VMEM((edges, width + ONES, block), F32),
            pltpu.VMEM((features, features), BF16),
            pltpu.VMEM((features, features), BF16),
            pltpu.VMEM((features, labels), BF16),
            pltpu.VMEM((slots, width, block), BF16),
            pltpu.VMEM((slots, width, block), BF16),
            pltpu.VMEM((subs, width, labels), BF16),
            pltpu.VMEM((features, labels), BF16),
            pltpu.VMEM((blocks, 8, block), F32),
            pltpu.VMEM((features, labels), BF16),
            pltpu.VMEM((features, labels), BF16),
            pltpu.VMEM((labels // block, features, block), BF16),
            pltpu.VMEM((half, features), BF16),
            pltpu.VMEM((half, features), F32),
            pltpu.VMEM((half, features), BF16),
            pltpu.VMEM((half, features), BF16),
            pltpu.VMEM((cols_x - 1, xrows, features), BF16),
            pltpu.VMEM((xrows, features), BF16),
            pltpu.VMEM((deep - 1, 16, features // 2), BF16),
            pltpu.VMEM((ROWS_Y, 16, features // 2), BF16),
            pltpu.VMEM((features, features), BF16),
            pltpu.VMEM((blocks, width, block), BF16),
            pltpu.VMEM((blocks, width, block), BF16),
            pltpu.VMEM((slots, width, block), BF16),
            pltpu.VMEM((slots, width, block), BF16),
            pltpu.VMEM((slots, width, block), F32),
            pltpu.VMEM((width, span), BF16),
            dma((10,)),
            dma((blocks,)),
            dma((2, offsets)),
            dma((2, offsets)),
            dma((2, subs)),
            dma((2, subs)),
            dma((2, 1)),
            dma((2, cols_x)),
            dma((2, deep)),
            dma((2, ROWS_Y)),
            dma((2, deep)),
            dma((2, cols_x)),
            dma((2, cols_x)),
        ],
        compiler_params=pltpu.CompilerParams(
            collective_id=0, has_side_effects=True, vmem_limit_bytes=48 * 1024 * 1024
        ),
    )(plan, feats, weight, edge_mask[0], cotangent)
    return (hidden, d_feats, d_weight.astype(F32))


def solution(mesh):
    cols_x = mesh.shape["sub"] // CORES
    return jax.shard_map(
        functools.partial(shards, cols_x),
        mesh=mesh,
        in_specs=(
            P("sub", "dom"),
            P(),
            P("dom", None),
            P("dom", None),
            P("dom", None, None, None),
            P("dom", None, None),
            P("dom", None),
            P(None, ("dom", "sub")),
        ),
        out_specs=(P(None, ("dom", "sub")), P("sub", "dom"), P()),
        check_vma=False,
    )
```

```python
import functools

import jax
import jax.numpy as jnp
from jax import lax
from jax.experimental import pallas as pl
from jax.experimental.pallas import tpu as pltpu
from jax.sharding import PartitionSpec as P

ROWS_Y = 8
CORES = 2
ONES = 16
VMEM_BYTES = 60 * 1024 * 1024
F32 = jnp.float32
BF16 = jnp.bfloat16
FAR_FIRST = {4: (2, 1, 3, 0), 2: (1, 0)}


def offset_of(position):
    return (position // 2 + 1) * (1 - 2 * (position % 2))


def order_by(keys, attributes, key_count):
    size = keys.shape[1]
    row = lax.broadcasted_iota(jnp.int32, (size, size), 0)
    lane = lax.broadcasted_iota(jnp.int32, (size, size), 1)

    def column(values):
        spread = jnp.broadcast_to(values, (size, size))
        return jnp.sum(jnp.where(row == lane, spread, 0.0), axis=1, keepdims=True)

    keys_column = column(keys)
    same = jnp.broadcast_to(keys, (size, size)) == keys_column
    less = jnp.broadcast_to(keys, (size, size)) < keys_column
    earlier = same & (lane < row)
    rank = jnp.sum(jnp.where(less | earlier, 1.0, 0.0), axis=1, keepdims=True)
    keep = jnp.minimum(jnp.sum(jnp.where(earlier, 1.0, 0.0), axis=1, keepdims=True), 1.0)
    hit = jnp.where(rank == lane.astype(F32), 1.0, 0.0)

    def placed(values):
        return jnp.sum(hit * values, axis=0, keepdims=True)

    wanted = lax.broadcasted_iota(jnp.int32, (size, key_count), 1).astype(F32)
    last = jnp.sum(jnp.where(keys_column <= wanted, 1.0, 0.0), axis=0, keepdims=True) - 1.0
    present = jnp.sum(jnp.where(keys_column == wanted, 1.0, 0.0), axis=0, keepdims=True)
    index_column = lax.broadcasted_iota(jnp.int32, (size, 1), 0).astype(F32)
    return (
        [placed(index_column)]
        + [placed(column(values)) for values in attributes]
        + [placed(keep), jnp.maximum(last, 0.0), jnp.minimum(present, 1.0)]
    )


def plan_kernel(blocks, table_len, list_ref, count_ref, dst_ref, src_ref, out_ref):
    _, offsets, capacity = list_ref.shape
    slots = offsets * capacity
    dst = dst_ref[...].astype(F32)
    src = src_ref[...].astype(F32)
    lane = lax.broadcasted_iota(jnp.int32, (1, slots), 1)
    listed = jnp.zeros((1, slots), jnp.int32)
    live = jnp.zeros((1, slots), jnp.int32)
    for j in range(offsets):
        for k in range(capacity):
            here = lane == j * capacity + k
            listed = jnp.where(here, list_ref[0, j, k], listed)
            live = jnp.where(here & (k < count_ref[0, j]), 1, live)
    owner = jnp.where(live == 1, listed, blocks).astype(F32)
    rows = (
        order_by(dst, [src], blocks)
        + order_by(src, [dst], table_len)
        + [listed.astype(F32)]
        + order_by(owner, [], blocks)
    )
    out_ref[...] = jnp.zeros_like(out_ref)
    for index, values in enumerate(rows):
        out_ref[index : index + 1, : values.shape[1]] = values.astype(jnp.int32)


def kernel(
    cols_x,
    plan,
    feats,
    weight,
    mask,
    cot,
    hidden,
    d_feats,
    d_weight,
    table,
    mask_int,
    mask_half,
    sums,
    w,
    wt,
    cot_v,
    outgoing,
    incoming,
    agg,
    full,
    scales,
    hid,
    d_pre,
    d_agg,
    dw_out,
    dw_own,
    core_in,
    x_out,
    x_in,
    z_out,
    z_in,
    y_all,
    summed,
    back,
    scaled,
    returning,
    returned,
    slot_sums,
    result,
    local_sem,
    tile_sem,
    perm_sem,
    ret_sem,
    a2a_sem,
    back_sem,
    core_sem,
    x_sem,
    z_sem,
    y_sem,
    gz_sem,
    gx_sem,
    gc_sem,
):
    width, span = feats.shape
    edges, block, _ = mask.shape
    features = weight.shape[0]
    blocks = span // block
    slots = returned.shape[0]
    offsets = perm_sem.shape[1]
    capacity = slots // offsets
    subs = cols_x * CORES
    per_sub = blocks // subs
    half = features // CORES
    xrows = half // cols_x
    doms = lax.axis_size("dom")
    deep = doms // ROWS_Y
    wide = features // 2

    dom, sub = lax.axis_index("dom"), lax.axis_index("sub")
    z, y = dom // ROWS_Y, dom % ROWS_Y
    x, core = sub // CORES, sub % CORES
    sibling = x * CORES + 1 - core

    def tile(index):
        return pl.ds(pl.multiple_of(index * block, block), block)

    def push(src, dst, sems, index, to_dom, to_sub):
        copy = pltpu.make_async_remote_copy(
            src_ref=src,
            dst_ref=dst,
            send_sem=sems.at[0, index],
            recv_sem=sems.at[1, index],
            device_id=(to_dom, to_sub),
            device_id_type=pl.DeviceIdType.MESH,
        )
        copy.start()
        return copy

    def fetch(src, dst, index):
        copy = pltpu.make_async_copy(src, dst, local_sem.at[index])
        copy.start()
        return copy

    in_dom = [lax.rem(dom + offset_of(j) + doms, doms) for j in range(offsets)]
    against = [lax.rem(dom - offset_of(j) + doms, doms) for j in range(offsets)]
    in_sub = [
        (o * CORES + d, lax.rem(x + o, cols_x) * CORES + lax.rem(core + d, CORES))
        for o in FAR_FIRST[cols_x]
        for d in range(CORES)
        if o or d
    ]
    in_x = [(o, lax.rem(x + o, cols_x)) for o in FAR_FIRST[cols_x] if o]
    in_z = [(o, lax.rem(z + o, deep)) for o in range(1, deep)]
    in_y = [(o, lax.rem(y + o, ROWS_Y)) for o in range(1, ROWS_Y)]

    def own_tile(b):
        return pltpu.make_async_copy(feats.at[:, tile(b)], table.at[b, :width], tile_sem.at[b])

    def start_tile(b, carry):
        own_tile(b).start()
        return carry

    lax.fori_loop(0, blocks, start_tile, 0)

    barrier = pltpu.get_barrier_semaphore()
    partners = (
        [(d, sub) for d in in_dom]
        + [(dom, s) for _, s in in_sub]
        + [(other * ROWS_Y + y, sub) for _, other in in_z]
        + [(z * ROWS_Y + other, sub) for _, other in in_y]
    )
    for partner in partners:
        pl.semaphore_signal(
            barrier, inc=1, device_id=partner, device_id_type=pl.DeviceIdType.MESH
        )

    quarter = edges // 4
    mask_in = [
        fetch(mask.at[pl.ds(i * quarter, quarter)], mask_int.at[pl.ds(i * quarter, quarter)], 1 + i)
        for i in range(4)
    ]
    w_in = fetch(weight, w, 5)
    cot_in = fetch(cot, cot_v, 6)

    def ones_below(t, carry):
        table[t, width:, :] = jnp.ones((ONES, block), BF16)
        return carry

    lax.fori_loop(0, blocks + slots, ones_below, 0)

    def wait_tile(b, carry):
        own_tile(b).wait()
        return carry

    lax.fori_loop(0, blocks, wait_tile, 0)
    for slot in range(slots):
        outgoing[slot] = table[plan[10, slot]][:width]
    pl.semaphore_wait(barrier, len(partners))

    sent = [
        push(
            outgoing.at[pl.ds(j * capacity, capacity)],
            incoming.at[pl.ds(j * capacity, capacity)],
            perm_sem,
            j,
            in_dom[j],
            sub,
        )
        for j in range(offsets)
    ]
    for i in range(4):
        mask_in[i].wait()

        def halve(e, carry):
            mask_half[e] = mask_int[e].astype(F32).astype(BF16)
            return carry

        lax.fori_loop(i * quarter, (i + 1) * quarter, halve, 0, unroll=2)
    w_in.wait()
    strip = features // 4
    for i in range(4):
        wt[:, i * strip : (i + 1) * strip] = w[i * strip : (i + 1) * strip, :].T
    for copy in sent:
        copy.wait_recv()
    table[blocks:, :width, :] = incoming[...]

    def forward(q, running):
        product = lax.dot_general(
            table[plan[1, q]],
            mask_half[plan[0, q]],
            (((1,), (1,)), ((), ())),
            preferred_element_type=F32,
        )
        running = running * plan[2, q].astype(F32) + product
        sums[q] = running
        return running

    lax.fori_loop(0, edges, forward, jnp.zeros((width + ONES, block), F32), unroll=4)

    def aggregate(s):
        def one(i, carry):
            b = s * per_sub + i
            total = sums[plan[3, b]] * plan[4, b].astype(F32)
            scale = lax.rsqrt(1.0 + total[width : width + 1])
            scales[b] = jnp.broadcast_to(scale, (8, block))
            own = table[b, :width, :].astype(F32)
            agg[s, :, tile(i)] = ((own + total[:width]) * scale).astype(BF16)
            return carry

        lax.fori_loop(0, per_sub, one, 0)

    own_rows = pl.ds(pl.multiple_of(sub * width, width), width)
    across = []
    for index, s in in_sub:
        aggregate(s)
        across.append(push(agg.at[s], full.at[own_rows], a2a_sem, index, dom, s))
    aggregate(sub)
    full[own_rows, :] = agg[sub]
    cot_in.wait()
    for copy in across:
        copy.wait_recv()

    def half_rows(i):
        return pl.ds(pl.multiple_of(i * half, half), half)

    def transform(i):
        rows = half_rows(i)
        pre = jnp.dot(w[rows, :], full[...], preferred_element_type=F32)
        gate = 1.0 / (1.0 + jnp.exp(-pre))
        hid[rows, :] = (pre * gate).astype(BF16)
        d_pre[rows, :] = (
            cot_v[rows, :].astype(F32) * gate * (1.0 + pre * (1.0 - gate))
        ).astype(BF16)

    def term(i):
        return lax.dot_general(
            d_pre[half_rows(i), :],
            full[...],
            (((1,), (1,)), ((), ())),
            preferred_element_type=F32,
        )

    transform(1 - core)
    dw_out[...] = term(1 - core).astype(BF16)
    to_core = push(dw_out, core_in, core_sem, 0, dom, sibling)
    transform(core)
    hid_out = fetch(hid, hidden, 7)
    dw_own[...] = term(core)

    def x_rows(i):
        return pl.ds(pl.multiple_of(i * xrows, xrows), xrows)

    to_core.wait_recv()

    def add_core(i, carry):
        total = dw_own[x_rows(i), :] + core_in[x_rows(i), :].astype(F32)
        dw_own[x_rows(i), :] = total
        x_out[x_rows(i), :] = total.astype(BF16)
        return carry

    lax.fori_loop(0, cols_x, add_core, 0)
    to_x = [
        push(x_out.at[x_rows(other)], x_in.at[o - 1], x_sem, o, dom, other * CORES + core)
        for o, other in in_x
    ]

    def gradient(i, carry):
        rows = half_rows(i)
        product = jnp.dot(wt[rows, :], d_pre[...], preferred_element_type=F32).astype(BF16)
        for k in range(per_sub):
            d_agg[k, rows, :] = product[:, k * block : (k + 1) * block]
        return carry

    lax.fori_loop(0, CORES, gradient, 0)

    def z_part(i):
        return (
            pl.ds(pl.multiple_of((i // 2) * 16, 16), 16),
            pl.ds(pl.multiple_of((i % 2) * wide, wide), wide),
        )

    for copy in to_x:
        copy.wait_recv()
    total = dw_own[x_rows(x), :]
    for o in range(cols_x - 1):
        total = total + x_in[o].astype(F32)
    dw_own[:xrows, :] = total
    z_out[...] = total.astype(BF16)
    to_z = [
        push(z_out.at[z_part(other)], z_in.at[o - 1], z_sem, o, other * ROWS_Y + y, sub)
        for o, other in in_z
    ]
    own_blocks = pl.ds(sub * per_sub, per_sub)
    backward = [
        push(
            d_agg.at[:, pl.ds(pl.multiple_of(s * width, width), width)],
            back.at[own_blocks],
            back_sem,
            index,
            dom,
            s,
        )
        for index, s in in_sub
    ]
    back[own_blocks] = d_agg[:, own_rows, :]
    for copy in to_z:
        copy.wait_recv()
    rows, columns = z_part(z)
    total = dw_own[rows, columns]
    for o in range(deep - 1):
        total = total + z_in[o].astype(F32)
    y_all[y] = total.astype(BF16)
    to_y = [
        push(y_all.at[y], y_all.at[y], y_sem, o, z * ROWS_Y + other, sub) for o, other in in_y
    ]
    for copy in to_y:
        copy.wait_recv()
    total = y_all[0].astype(F32)
    for other in range(1, ROWS_Y):
        total = total + y_all[other].astype(F32)
    summed[...] = total.astype(BF16)

    def x_strip(of_core, of_x):
        return pl.ds(pl.multiple_of(of_core * half + of_x * xrows, xrows), xrows)

    mine = (
        pl.ds(pl.multiple_of(core * half + x * xrows + (z // 2) * 16, 16), 16),
        pl.ds(pl.multiple_of((z % 2) * wide, wide), wide),
    )
    over_z = [
        push(summed, d_weight.at[mine], gz_sem, o, other * ROWS_Y + y, sub) for o, other in in_z
    ]
    own_piece = fetch(summed, d_weight.at[mine], 0)
    for copy in backward:
        copy.wait_recv()

    def rescale(b, carry):
        scaled[b] = (back[b].astype(F32) * scales[b][:1]).astype(BF16)
        return carry

    lax.fori_loop(0, blocks, rescale, 0, unroll=2)
    def backward_edge(q, running):
        product = jnp.dot(
            scaled[plan[6, q]], mask_half[plan[5, q]], preferred_element_type=F32
        )
        running = running * plan[7, q].astype(F32) + product
        sums[q, :width, :] = running
        return running

    lax.fori_loop(0, edges, backward_edge, jnp.zeros((width, block), F32), unroll=4)
    home = []
    for j in range(offsets):
        for k in range(capacity):
            t = blocks + j * capacity + k
            returning[j * capacity + k] = (
                sums[plan[8, t]][:width] * plan[9, t].astype(F32)
            ).astype(BF16)
        home.append(
            push(
                returning.at[pl.ds(j * capacity, capacity)],
                returned.at[pl.ds(j * capacity, capacity)],
                ret_sem,
                j,
                against[j],
                sub,
            )
        )
    for copy in over_z:
        copy.wait_recv()
    own_piece.wait()
    strip_x = d_weight.at[x_strip(core, x)]
    over_x = [
        push(strip_x, strip_x, gx_sem, o, dom, other * CORES + core) for o, other in in_x
    ]
    over_core = [push(strip_x, strip_x, gc_sem, 0, dom, sibling)]
    for copy in home:
        copy.wait_recv()

    def add_slot(i, running):
        running = running * plan[12, i].astype(F32) + returned[plan[11, i]].astype(F32)
        slot_sums[i] = running
        return running

    lax.fori_loop(0, slots, add_slot, jnp.zeros((width, block), F32))

    def finish(b, carry):
        result[:, tile(b)] = (
            scaled[b].astype(F32)
            + sums[plan[8, b]][:width] * plan[9, b].astype(F32)
            + slot_sums[plan[13, b]] * plan[14, b].astype(F32)
        ).astype(BF16)
        return carry

    lax.fori_loop(0, blocks, finish, 0, unroll=2)
    d_feats_out = fetch(result, d_feats, 8)
    for (o, _), copy in zip(in_x, over_x):
        copy.wait_recv()
        arrived = d_weight.at[x_strip(core, lax.rem(x - o + cols_x, cols_x))]
        over_core.append(push(arrived, arrived, gc_sem, o, dom, sibling))
    for copy in over_core:
        copy.wait_recv()
    for copy in (
        sent
        + across
        + [to_core]
        + to_x
        + backward
        + to_z
        + to_y
        + home
        + over_z
        + over_x
        + over_core
    ):
        copy.wait_send()
    hid_out.wait()
    d_feats_out.wait()


def write_kernel(
    hid, d_feats, d_weight, hid_out, d_feats_out, d_weight_out, narrow, wide, sem, part_sem
):
    parts, rows, _ = narrow.shape
    whole = [
        pltpu.make_async_copy(hid, hid_out, sem.at[0]),
        pltpu.make_async_copy(d_feats, d_feats_out, sem.at[1]),
    ]
    spans = [pl.ds(i * rows, rows) for i in range(parts)]
    into = [
        pltpu.make_async_copy(d_weight.at[spans[i]], narrow.at[i], part_sem.at[0, i])
        for i in range(parts)
    ]
    out_of = [
        pltpu.make_async_copy(wide.at[i], d_weight_out.at[spans[i]], part_sem.at[1, i])
        for i in range(parts)
    ]
    for copy in into + whole:
        copy.start()
    for i in range(parts):
        into[i].wait()
        wide[i] = narrow[i].astype(F32)
        out_of[i].start()
    for copy in out_of + whole:
        copy.wait()


def shards(cols_x, feats, weight, edge_dst, edge_src, edge_mask, send_list, send_count, cotangent):
    width, span = feats.shape
    _, edges, block, _ = edge_mask.shape
    features = weight.shape[0]
    blocks = span // block
    _, offsets, capacity = send_list.shape
    slots = offsets * capacity
    table_len = blocks + slots
    subs = cols_x * CORES
    labels = span // subs
    half = features // CORES
    xrows = half // cols_x
    deep = lax.axis_size("dom") // ROWS_Y
    vmem, smem, hbm, anywhere = (
        pl.BlockSpec(memory_space=space) for space in (pltpu.VMEM, pltpu.SMEM, pltpu.HBM, pl.ANY)
    )
    plan = pl.pallas_call(
        functools.partial(plan_kernel, blocks, table_len),
        out_shape=jax.ShapeDtypeStruct((16, 128), jnp.int32),
        in_specs=[smem, smem, vmem, vmem],
        out_specs=vmem,
        compiler_params=pltpu.CompilerParams(vmem_limit_bytes=VMEM_BYTES),
    )(send_list, send_count, edge_dst, edge_src)
    dma = pltpu.SemaphoreType.DMA
    hidden, d_feats, d_weight = pl.pallas_call(
        functools.partial(kernel, cols_x),
        out_shape=(
            jax.ShapeDtypeStruct((features, labels), BF16),
            jax.ShapeDtypeStruct((width, span), BF16),
            jax.ShapeDtypeStruct((features, features), BF16),
        ),
        in_specs=[smem] + [hbm] * 4,
        out_specs=(anywhere,) * 3,
        scratch_shapes=[
            pltpu.VMEM((table_len, width + ONES, block), BF16),
            pltpu.VMEM((edges, block, block), jnp.int32),
            pltpu.VMEM((edges, block, block), BF16),
            pltpu.VMEM((edges, width + ONES, block), F32),
            pltpu.VMEM((features, features), BF16),
            pltpu.VMEM((features, features), BF16),
            pltpu.VMEM((features, labels), BF16),
            pltpu.VMEM((slots, width, block), BF16),
            pltpu.VMEM((slots, width, block), BF16),
            pltpu.VMEM((subs, width, labels), BF16),
            pltpu.VMEM((features, labels), BF16),
            pltpu.VMEM((blocks, 8, block), F32),
            pltpu.VMEM((features, labels), BF16),
            pltpu.VMEM((features, labels), BF16),
            pltpu.VMEM((labels // block, features, block), BF16),
            pltpu.VMEM((half, features), BF16),
            pltpu.VMEM((half, features), F32),
            pltpu.VMEM((half, features), BF16),
            pltpu.VMEM((half, features), BF16),
            pltpu.VMEM((cols_x - 1, xrows, features), BF16),
            pltpu.VMEM((xrows, features), BF16),
            pltpu.VMEM((deep - 1, 16, features // 2), BF16),
            pltpu.VMEM((ROWS_Y, 16, features // 2), BF16),
            pltpu.VMEM((16, features // 2), BF16),
            pltpu.VMEM((blocks, width, block), BF16),
            pltpu.VMEM((blocks, width, block), BF16),
            pltpu.VMEM((slots, width, block), BF16),
            pltpu.VMEM((slots, width, block), BF16),
            pltpu.VMEM((slots, width, block), F32),
            pltpu.VMEM((width, span), BF16),
            dma((10,)),
            dma((blocks,)),
            dma((2, offsets)),
            dma((2, offsets)),
            dma((2, subs)),
            dma((2, subs)),
            dma((2, 1)),
            dma((2, cols_x)),
            dma((2, deep)),
            dma((2, ROWS_Y)),
            dma((2, deep)),
            dma((2, cols_x)),
            dma((2, cols_x)),
        ],
        compiler_params=pltpu.CompilerParams(
            collective_id=0, has_side_effects=True, vmem_limit_bytes=VMEM_BYTES
        ),
    )(plan, feats, weight, edge_mask[0], cotangent)
    return pl.pallas_call(
        write_kernel,
        out_shape=(
            jax.ShapeDtypeStruct((features, labels), BF16),
            jax.ShapeDtypeStruct((width, span), BF16),
            jax.ShapeDtypeStruct((features, features), F32),
        ),
        in_specs=[anywhere] * 3,
        out_specs=(hbm,) * 3,
        scratch_shapes=[
            pltpu.VMEM((4, features // 4, features), BF16),
            pltpu.VMEM((4, features // 4, features), F32),
            dma((2,)),
            dma((2, 4)),
        ],
        compiler_params=pltpu.CompilerParams(vmem_limit_bytes=VMEM_BYTES),
    )(hidden, d_feats, d_weight)


def solution(mesh):
    cols_x = mesh.shape["sub"] // CORES
    return jax.shard_map(
        functools.partial(shards, cols_x),
        mesh=mesh,
        in_specs=(
            P("sub", "dom"),
            P(),
            P("dom", None),
            P("dom", None),
            P("dom", None, None, None),
            P("dom", None, None),
            P("dom", None),
            P(None, ("dom", "sub")),
        ),
        out_specs=(P(None, ("dom", "sub")), P("sub", "dom"), P()),
        check_vma=False,
    )
```

```python
import functools

import jax
import jax.numpy as jnp
from jax import lax
from jax.experimental import pallas as pl
from jax.experimental.pallas import tpu as pltpu
from jax.sharding import PartitionSpec as P

ROWS_Y = 8
CORES = 2
ONES = 16
TALL = 16
SECOND_PAIRS = 4
VMEM_BYTES = 60 * 1024 * 1024
F32 = jnp.float32
BF16 = jnp.bfloat16
FAR_FIRST = {4: (2, 1, 3, 0), 2: (1, 0)}


def offset_of(position):
    return (position // 2 + 1) * (1 - 2 * (position % 2))


def order_by(keys, attributes, key_count):
    size = keys.shape[1]
    row = lax.broadcasted_iota(jnp.int32, (size, size), 0)
    lane = lax.broadcasted_iota(jnp.int32, (size, size), 1)

    def column(values):
        spread = jnp.broadcast_to(values, (size, size))
        return jnp.sum(jnp.where(row == lane, spread, 0.0), axis=1, keepdims=True)

    keys_column = column(keys)
    same = jnp.broadcast_to(keys, (size, size)) == keys_column
    less = jnp.broadcast_to(keys, (size, size)) < keys_column
    earlier = same & (lane < row)
    rank = jnp.sum(jnp.where(less | earlier, 1.0, 0.0), axis=1, keepdims=True)
    keep = jnp.minimum(jnp.sum(jnp.where(earlier, 1.0, 0.0), axis=1, keepdims=True), 1.0)
    hit = jnp.where(rank == lane.astype(F32), 1.0, 0.0)

    def placed(values):
        return jnp.sum(hit * values, axis=0, keepdims=True)

    wanted = lax.broadcasted_iota(jnp.int32, (size, key_count), 1).astype(F32)
    last = jnp.sum(jnp.where(keys_column <= wanted, 1.0, 0.0), axis=0, keepdims=True) - 1.0
    present = jnp.sum(jnp.where(keys_column == wanted, 1.0, 0.0), axis=0, keepdims=True)
    index_column = lax.broadcasted_iota(jnp.int32, (size, 1), 0).astype(F32)
    return (
        [placed(index_column)]
        + [placed(column(values)) for values in attributes]
        + [placed(keep), jnp.maximum(last, 0.0), jnp.minimum(present, 1.0)]
    )


def plan_kernel(blocks, table_len, list_ref, count_ref, dst_ref, src_ref, out_ref):
    _, offsets, capacity = list_ref.shape
    slots = offsets * capacity
    dst = dst_ref[...].astype(F32)
    src = src_ref[...].astype(F32)
    lane = lax.broadcasted_iota(jnp.int32, (1, slots), 1)
    listed = jnp.zeros((1, slots), jnp.int32)
    live = jnp.zeros((1, slots), jnp.int32)
    for j in range(offsets):
        for k in range(capacity):
            here = lane == j * capacity + k
            listed = jnp.where(here, list_ref[0, j, k], listed)
            live = jnp.where(here & (k < count_ref[0, j]), 1, live)
    owner = jnp.where(live == 1, listed, blocks).astype(F32)
    rows = (
        order_by(dst, [src], blocks)
        + order_by(src, [dst], table_len)
        + [listed.astype(F32)]
        + order_by(owner, [], blocks)
    )
    out_ref[...] = jnp.zeros_like(out_ref)
    for index, values in enumerate(rows):
        out_ref[index : index + 1, : values.shape[1]] = values.astype(jnp.int32)


def kernel(
    cols_x,
    plan,
    feats,
    weight,
    mask,
    cot,
    hidden,
    d_feats,
    d_weight,
    table,
    mask_int,
    mask_half,
    sums,
    w,
    wt,
    cot_v,
    outgoing,
    incoming,
    agg,
    full,
    scales,
    hid,
    d_pre,
    d_agg,
    dw_out,
    dw_own,
    core_in,
    half_out,
    y1_in,
    z1_in,
    first,
    second,
    z2_out,
    z2_in,
    x2_out,
    x2_in,
    x3_all,
    y3_all,
    line,
    square,
    gathered,
    back,
    scaled,
    returning,
    returned,
    slot_sums,
    result,
    local_sem,
    tile_sem,
    perm_sem,
    ret_sem,
    a2a_sem,
    back_sem,
    core_sem,
    y1_sem,
    z1_sem,
    x2_sem,
    z2_sem,
    x3_sem,
    y3_sem,
    x4_sem,
    z4_sem,
    y5_sem,
    z5_sem,
    x6_sem,
    gc_sem,
):
    width, span = feats.shape
    edges, block, _ = mask.shape
    features = weight.shape[0]
    blocks = span // block
    slots = returned.shape[0]
    offsets = perm_sem.shape[1]
    capacity = slots // offsets
    subs = cols_x * CORES
    per_sub = blocks // subs
    half = features // CORES
    doms = lax.axis_size("dom")
    deep = doms // ROWS_Y
    wide = features // 2
    row_z, across_z = deep // 2, deep // 4
    lanes = features // row_z

    dom, sub = lax.axis_index("dom"), lax.axis_index("sub")
    z, y = dom // ROWS_Y, dom % ROWS_Y
    x, core = sub // CORES, sub % CORES
    sibling = x * CORES + 1 - core

    def tile(index):
        return pl.ds(pl.multiple_of(index * block, block), block)

    def push(src, dst, sems, index, to_dom, to_sub):
        copy = pltpu.make_async_remote_copy(
            src_ref=src,
            dst_ref=dst,
            send_sem=sems.at[0, index],
            recv_sem=sems.at[1, index],
            device_id=(to_dom, to_sub),
            device_id_type=pl.DeviceIdType.MESH,
        )
        copy.start()
        return copy

    def fetch(src, dst, index):
        copy = pltpu.make_async_copy(src, dst, local_sem.at[index])
        copy.start()
        return copy

    in_dom = [lax.rem(dom + offset_of(j) + doms, doms) for j in range(offsets)]
    against = [lax.rem(dom - offset_of(j) + doms, doms) for j in range(offsets)]
    in_sub = [
        (o * CORES + d, lax.rem(x + o, cols_x) * CORES + lax.rem(core + d, CORES))
        for o in FAR_FIRST[cols_x]
        for d in range(CORES)
        if o or d
    ]
    in_x = [(o, lax.rem(x + o, cols_x)) for o in FAR_FIRST[cols_x] if o]
    in_z = [(o, lax.rem(z + o, deep)) for o in range(1, deep)]
    in_y = [(o, lax.rem(y + o, ROWS_Y)) for o in range(1, ROWS_Y)]

    def own_tile(b):
        return pltpu.make_async_copy(feats.at[:, tile(b)], table.at[b, :width], tile_sem.at[b])

    def start_tile(b, carry):
        own_tile(b).start()
        return carry

    lax.fori_loop(0, blocks, start_tile, 0)

    barrier = pltpu.get_barrier_semaphore()
    partners = (
        [(d, sub) for d in in_dom]
        + [(dom, s) for _, s in in_sub]
        + [(other * ROWS_Y + y, sub) for _, other in in_z]
        + [(z * ROWS_Y + other, sub) for _, other in in_y]
    )
    for partner in partners:
        pl.semaphore_signal(
            barrier, inc=1, device_id=partner, device_id_type=pl.DeviceIdType.MESH
        )

    quarter = edges // 4
    mask_in = [
        fetch(mask.at[pl.ds(i * quarter, quarter)], mask_int.at[pl.ds(i * quarter, quarter)], 1 + i)
        for i in range(4)
    ]
    w_in = fetch(weight, w, 5)
    cot_in = fetch(cot, cot_v, 6)

    def ones_below(t, carry):
        table[t, width:, :] = jnp.ones((ONES, block), BF16)
        return carry

    lax.fori_loop(0, blocks + slots, ones_below, 0)

    def wait_tile(b, carry):
        own_tile(b).wait()
        return carry

    lax.fori_loop(0, blocks, wait_tile, 0)
    for slot in range(slots):
        outgoing[slot] = table[plan[10, slot]][:width]
    pl.semaphore_wait(barrier, len(partners))

    sent = [
        push(
            outgoing.at[pl.ds(j * capacity, capacity)],
            incoming.at[pl.ds(j * capacity, capacity)],
            perm_sem,
            j,
            in_dom[j],
            sub,
        )
        for j in range(offsets)
    ]
    for i in range(4):
        mask_in[i].wait()

        def halve(e, carry):
            mask_half[e] = mask_int[e].astype(F32).astype(BF16)
            return carry

        lax.fori_loop(i * quarter, (i + 1) * quarter, halve, 0, unroll=2)
    w_in.wait()
    strip = features // 4
    for i in range(4):
        wt[:, i * strip : (i + 1) * strip] = w[i * strip : (i + 1) * strip, :].T
    for copy in sent:
        copy.wait_recv()
    table[blocks:, :width, :] = incoming[...]

    def forward(q, running):
        product = lax.dot_general(
            table[plan[1, q]],
            mask_half[plan[0, q]],
            (((1,), (1,)), ((), ())),
            preferred_element_type=F32,
        )
        running = running * plan[2, q].astype(F32) + product
        sums[q] = running
        return running

    lax.fori_loop(0, edges, forward, jnp.zeros((width + ONES, block), F32), unroll=4)

    def aggregate(s):
        def one(i, carry):
            b = s * per_sub + i
            total = sums[plan[3, b]] * plan[4, b].astype(F32)
            scale = lax.rsqrt(1.0 + total[width : width + 1])
            scales[b] = jnp.broadcast_to(scale, (8, block))
            own = table[b, :width, :].astype(F32)
            agg[s, :, tile(i)] = ((own + total[:width]) * scale).astype(BF16)
            return carry

        lax.fori_loop(0, per_sub, one, 0)

    own_rows = pl.ds(pl.multiple_of(sub * width, width), width)
    across = []
    for index, s in in_sub:
        aggregate(s)
        across.append(push(agg.at[s], full.at[own_rows], a2a_sem, index, dom, s))
    aggregate(sub)
    full[own_rows, :] = agg[sub]
    cot_in.wait()
    for copy in across:
        copy.wait_recv()

    def half_rows(i):
        return pl.ds(pl.multiple_of(i * half, half), half)

    def transform(i):
        rows = half_rows(i)
        pre = jnp.dot(w[rows, :], full[...], preferred_element_type=F32)
        gate = 1.0 / (1.0 + jnp.exp(-pre))
        hid[rows, :] = (pre * gate).astype(BF16)
        d_pre[rows, :] = (
            cot_v[rows, :].astype(F32) * gate * (1.0 + pre * (1.0 - gate))
        ).astype(BF16)

    def term(i):
        return lax.dot_general(
            d_pre[half_rows(i), :],
            full[...],
            (((1,), (1,)), ((), ())),
            preferred_element_type=F32,
        )

    transform(1 - core)
    dw_out[...] = term(1 - core).astype(BF16)
    to_core = push(dw_out, core_in, core_sem, 0, dom, sibling)
    transform(core)
    hid_out = fetch(hid, hidden, 7)

    def gradient(i, carry):
        rows = half_rows(i)
        product = jnp.dot(wt[rows, :], d_pre[...], preferred_element_type=F32).astype(BF16)
        for k in range(per_sub):
            d_agg[k, rows, :] = product[:, k * block : (k + 1) * block]
        return carry

    lax.fori_loop(0, CORES, gradient, 0)
    own_blocks = pl.ds(sub * per_sub, per_sub)
    backward = [
        push(
            d_agg.at[:, pl.ds(pl.multiple_of(s * width, width), width)],
            back.at[own_blocks],
            back_sem,
            index,
            dom,
            s,
        )
        for index, s in in_sub
    ]
    back[own_blocks] = d_agg[:, own_rows, :]
    dw_own[...] = term(core)
    to_core.wait_recv()

    def add_core(i, carry):
        rows = pl.ds(pl.multiple_of(i * 2 * TALL, 2 * TALL), 2 * TALL)
        total = dw_own[rows, :] + core_in[rows, :].astype(F32)
        dw_own[rows, :] = total
        half_out[rows, :] = total.astype(BF16)
        return carry

    lax.fori_loop(0, half // (2 * TALL), add_core, 0)

    def first_part(i):
        return pl.ds(pl.multiple_of(i * 2 * TALL, 2 * TALL), 2 * TALL), slice(None)

    def second_part(i):
        return (
            pl.ds(pl.multiple_of(ROWS_Y * 2 * TALL + (i // across_z) * 2 * TALL, 2 * TALL), 2 * TALL),
            pl.ds(pl.multiple_of((i % across_z) * 2 * lanes, 2 * lanes), 2 * lanes),
        )

    def one_tile(i, in_row):
        return (
            i // in_row,
            slice(None),
            pl.ds(pl.multiple_of((i % in_row) * lanes, lanes), lanes),
        )

    def tall_tile(i, in_row):
        return (
            pl.ds(pl.multiple_of((i // in_row) * TALL, TALL), TALL),
            pl.ds(pl.multiple_of((i % in_row) * lanes, lanes), lanes),
        )

    def over_z(src_of, dst_of, sems):
        return [
            push(src_of(other), dst_of(o), sems, o, other * ROWS_Y + y, sub) for o, other in in_z
        ]

    def over_y(src_of, dst_of, sems):
        return [
            push(src_of(other), dst_of(o), sems, o, z * ROWS_Y + other, sub) for o, other in in_y
        ]

    def over_x(src_of, dst_of, sems):
        return [
            push(src_of(other), dst_of(o), sems, o, dom, other * CORES + core)
            for o, other in in_x
        ]

    def arrive(copies):
        for copy in copies:
            copy.wait_recv()

    y1 = over_y(lambda i: half_out.at[first_part(i)], lambda o: y1_in.at[o - 1], y1_sem)
    z1 = over_z(lambda i: half_out.at[second_part(i)], lambda o: z1_in.at[o - 1], z1_sem)
    arrive(z1)
    total = dw_own[second_part(z)]
    for o in range(deep - 1):
        total = total + z1_in[o].astype(F32)
    second[...] = total
    for i in range(2):
        x2_out[i] = total[i * TALL : (i + 1) * TALL].astype(BF16)
    x2 = over_x(lambda i: x2_out.at[one_tile(i, 2)], lambda o: x2_in.at[o - 1], x2_sem)
    arrive(y1)
    total = dw_own[first_part(y)]
    for o in range(ROWS_Y - 1):
        total = total + y1_in[o].astype(F32)
    first[...] = total
    for i in range(2):
        z2_out[i] = total[i * TALL : (i + 1) * TALL].astype(BF16)
    z2 = over_z(lambda i: z2_out.at[one_tile(i, row_z)], lambda o: z2_in.at[o - 1], z2_sem)
    arrive(backward)

    def rescale(b, carry):
        scaled[b] = (back[b].astype(F32) * scales[b][:1]).astype(BF16)
        return carry

    lax.fori_loop(0, blocks, rescale, 0, unroll=2)

    def backward_edge(q, running):
        product = jnp.dot(scaled[plan[6, q]], mask_half[plan[5, q]], preferred_element_type=F32)
        running = running * plan[7, q].astype(F32) + product
        sums[q, :width, :] = running
        return running

    running = lax.fori_loop(
        0, edges // 2, backward_edge, jnp.zeros((width, block), F32), unroll=4
    )
    arrive(x2)
    total = second[tall_tile(x, 2)]
    for o in range(cols_x - 1):
        total = total + x2_in[o].astype(F32)
    y3_all[y] = total.astype(BF16)
    y3 = over_y(lambda i: y3_all.at[y], lambda o: y3_all.at[y], y3_sem)
    arrive(z2)
    total = first[tall_tile(z, row_z)]
    for o in range(deep - 1):
        total = total + z2_in[o].astype(F32)
    x3_all[x] = total.astype(BF16)
    x3 = over_x(lambda i: x3_all.at[x], lambda o: x3_all.at[x], x3_sem)
    lax.fori_loop(edges // 2, edges, backward_edge, running, unroll=4)
    home = []
    for j in range(offsets):
        for k in range(capacity):
            t = blocks + j * capacity + k
            returning[j * capacity + k] = (
                sums[plan[8, t]][:width] * plan[9, t].astype(F32)
            ).astype(BF16)
        home.append(
            push(
                returning.at[pl.ds(j * capacity, capacity)],
                returned.at[pl.ds(j * capacity, capacity)],
                ret_sem,
                j,
                against[j],
                sub,
            )
        )
    arrive(x3)
    total = x3_all[0].astype(F32)
    for other in range(1, cols_x):
        total = total + x3_all[other].astype(F32)
    mine = one_tile(z, row_z)
    line[mine] = total.astype(BF16)
    z4 = over_z(lambda i: line.at[mine], lambda o: line.at[mine], z4_sem)
    arrive(y3)
    total = y3_all[0].astype(F32)
    for other in range(1, ROWS_Y):
        total = total + y3_all[other].astype(F32)
    own_tile_x = one_tile(x, 2)
    square[own_tile_x] = total.astype(BF16)
    x4 = over_x(lambda i: square.at[own_tile_x], lambda o: square.at[own_tile_x], x4_sem)
    quarter_of = [
        (i // 2, slice(None), pl.ds(pl.multiple_of((i % 2) * wide, wide), wide))
        for i in (x, *(lax.rem(x - o + cols_x, cols_x) for o, _ in in_x))
    ]
    arrive(x4)
    square_at = (
        core,
        ROWS_Y + z // across_z,
        slice(None),
        slice(None),
        pl.ds(pl.multiple_of((z % across_z) * 2 * lanes, 2 * lanes), 2 * lanes),
    )
    gathered[square_at] = square[...]
    z5 = over_z(lambda i: square, lambda o: gathered.at[square_at], z5_sem)
    arrive(z4)
    own_quarter = quarter_of[0]
    gathered[(core, y) + own_quarter] = line[own_quarter]
    y5 = over_y(
        lambda i: line.at[own_quarter],
        lambda o: gathered.at[(core, y) + own_quarter],
        y5_sem,
    )

    def all_y(quarter):
        return gathered.at[(core, pl.ds(0, ROWS_Y)) + quarter]

    arrive(y5)
    x6 = over_x(lambda i: all_y(own_quarter), lambda o: all_y(own_quarter), x6_sem)
    to_sibling = [push(all_y(own_quarter), all_y(own_quarter), gc_sem, 0, dom, sibling)]
    arrive(home)

    def add_slot(i, running):
        running = running * plan[12, i].astype(F32) + returned[plan[11, i]].astype(F32)
        slot_sums[i] = running
        return running

    lax.fori_loop(0, slots, add_slot, jnp.zeros((width, block), F32))

    def finish(b, carry):
        result[:, tile(b)] = (
            scaled[b].astype(F32)
            + sums[plan[8, b]][:width] * plan[9, b].astype(F32)
            + slot_sums[plan[13, b]] * plan[14, b].astype(F32)
        ).astype(BF16)
        return carry

    lax.fori_loop(0, blocks, finish, 0, unroll=2)
    d_feats_out = fetch(result, d_feats, 8)
    arrive(z5)
    last_rows = gathered.at[core, pl.ds(ROWS_Y, SECOND_PAIRS)]
    to_sibling.append(push(last_rows, last_rows, gc_sem, cols_x, dom, sibling))
    for (o, _), copy, quarter in zip(in_x, x6, quarter_of[1:]):
        copy.wait_recv()
        to_sibling.append(push(all_y(quarter), all_y(quarter), gc_sem, o, dom, sibling))
    arrive(to_sibling)
    d_weight_out = fetch(gathered, d_weight, 9)
    for copies in (
        sent, across, [to_core], backward, y1, z1, x2, z2, x3, y3, home, x4, z4, y5, z5, x6, to_sibling
    ):
        for copy in copies:
            copy.wait_send()
    hid_out.wait()
    d_feats_out.wait()
    d_weight_out.wait()


def write_kernel(
    hid, d_feats, d_weight, hid_out, d_feats_out, d_weight_out, hid_v, d_feats_v, narrow, wide, sem
):
    parts, pairs, _, _, features = narrow.shape
    per_core = d_weight.shape[1] // pairs
    rows = features // parts
    columns = d_feats_v.shape[2]
    out_of = []
    into = []
    for i in range(parts):
        span, lanes = pl.ds(i * rows, rows), pl.ds(i * columns, columns)
        steps = (
            (
                d_weight.at[i // per_core, pl.ds((i % per_core) * pairs, pairs)],
                narrow.at[i],
                wide.at[i],
                d_weight_out.at[span],
            ),
            (hid.at[span], hid_v.at[i], hid_v.at[i], hid_out.at[span]),
            (d_feats.at[:, lanes], d_feats_v.at[i], d_feats_v.at[i], d_feats_out.at[:, lanes]),
        )
        for j, (here, arrive, leave, there) in enumerate(steps):
            into.append(pltpu.make_async_copy(here, arrive, sem.at[0, 3 * i + j]))
            out_of.append(pltpu.make_async_copy(leave, there, sem.at[1, 3 * i + j]))
    for copy in into:
        copy.start()
    for i in range(parts):
        for j in range(3):
            into[3 * i + j].wait()
            if j == 0:
                wide[i] = narrow[i].astype(F32).reshape(rows, features)
            out_of[3 * i + j].start()
    for copy in out_of:
        copy.wait()


def shards(cols_x, feats, weight, edge_dst, edge_src, edge_mask, send_list, send_count, cotangent):
    width, span = feats.shape
    _, edges, block, _ = edge_mask.shape
    features = weight.shape[0]
    blocks = span // block
    _, offsets, capacity = send_list.shape
    slots = offsets * capacity
    table_len = blocks + slots
    subs = cols_x * CORES
    labels = span // subs
    half = features // CORES
    deep = lax.axis_size("dom") // ROWS_Y
    lanes = features // (deep // 2)
    gather_shape = (CORES, ROWS_Y + SECOND_PAIRS, 2, TALL, features)
    vmem, smem, hbm, anywhere = (
        pl.BlockSpec(memory_space=space) for space in (pltpu.VMEM, pltpu.SMEM, pltpu.HBM, pl.ANY)
    )
    plan = pl.pallas_call(
        functools.partial(plan_kernel, blocks, table_len),
        out_shape=jax.ShapeDtypeStruct((16, 128), jnp.int32),
        in_specs=[smem, smem, vmem, vmem],
        out_specs=vmem,
        compiler_params=pltpu.CompilerParams(vmem_limit_bytes=VMEM_BYTES),
    )(send_list, send_count, edge_dst, edge_src)
    dma = pltpu.SemaphoreType.DMA
    hidden, d_feats, d_weight = pl.pallas_call(
        functools.partial(kernel, cols_x),
        out_shape=(
            jax.ShapeDtypeStruct((features, labels), BF16),
            jax.ShapeDtypeStruct((width, span), BF16),
            jax.ShapeDtypeStruct(gather_shape, BF16),
        ),
        in_specs=[smem] + [hbm] * 4,
        out_specs=(anywhere,) * 3,
        scratch_shapes=[
            pltpu.VMEM((table_len, width + ONES, block), BF16),
            pltpu.VMEM((edges, block, block), jnp.int32),
            pltpu.VMEM((edges, block, block), BF16),
            pltpu.VMEM((edges, width + ONES, block), F32),
            pltpu.VMEM((features, features), BF16),
            pltpu.VMEM((features, features), BF16),
            pltpu.VMEM((features, labels), BF16),
            pltpu.VMEM((slots, width, block), BF16),
            pltpu.VMEM((slots, width, block), BF16),
            pltpu.VMEM((subs, width, labels), BF16),
            pltpu.VMEM((features, labels), BF16),
            pltpu.VMEM((blocks, 8, block), F32),
            pltpu.VMEM((features, labels), BF16),
            pltpu.VMEM((features, labels), BF16),
            pltpu.VMEM((labels // block, features, block), BF16),
            pltpu.VMEM((half, features), BF16),
            pltpu.VMEM((half, features), F32),
            pltpu.VMEM((half, features), BF16),
            pltpu.VMEM((half, features), BF16),
            pltpu.VMEM((ROWS_Y - 1, 2 * TALL, features), BF16),
            pltpu.VMEM((deep - 1, 2 * TALL, 2 * lanes), BF16),
            pltpu.VMEM((2 * TALL, features), F32),
            pltpu.VMEM((2 * TALL, 2 * lanes), F32),
            pltpu.VMEM((2, TALL, features), BF16),
            pltpu.VMEM((deep - 1, TALL, lanes), BF16),
            pltpu.VMEM((2, TALL, 2 * lanes), BF16),
            pltpu.VMEM((cols_x - 1, TALL, lanes), BF16),
            pltpu.VMEM((cols_x, TALL, lanes), BF16),
            pltpu.VMEM((ROWS_Y, TALL, lanes), BF16),
            pltpu.VMEM((2, TALL, features), BF16),
            pltpu.VMEM((2, TALL, 2 * lanes), BF16),
            pltpu.VMEM(gather_shape, BF16),
            pltpu.VMEM((blocks, width, block), BF16),
            pltpu.VMEM((blocks, width, block), BF16),
            pltpu.VMEM((slots, width, block), BF16),
            pltpu.VMEM((slots, width, block), BF16),
            pltpu.VMEM((slots, width, block), F32),
            pltpu.VMEM((width, span), BF16),
            dma((10,)),
            dma((blocks,)),
            dma((2, offsets)),
            dma((2, offsets)),
            dma((2, subs)),
            dma((2, subs)),
            dma((2, 1)),
            dma((2, ROWS_Y)),
            dma((2, deep)),
            dma((2, cols_x)),
            dma((2, deep)),
            dma((2, cols_x)),
            dma((2, ROWS_Y)),
            dma((2, cols_x)),
            dma((2, deep)),
            dma((2, ROWS_Y)),
            dma((2, deep)),
            dma((2, cols_x)),
            dma((2, cols_x + 1)),
        ],
        compiler_params=pltpu.CompilerParams(
            collective_id=0, has_side_effects=True, vmem_limit_bytes=VMEM_BYTES
        ),
    )(plan, feats, weight, edge_mask[0], cotangent)
    return pl.pallas_call(
        write_kernel,
        out_shape=(
            jax.ShapeDtypeStruct((features, labels), BF16),
            jax.ShapeDtypeStruct((width, span), BF16),
            jax.ShapeDtypeStruct((features, features), F32),
        ),
        in_specs=[anywhere] * 3,
        out_specs=(hbm,) * 3,
        scratch_shapes=[
            pltpu.VMEM((4, features // 4, labels), BF16),
            pltpu.VMEM((4, width, span // 4), BF16),
            pltpu.VMEM((4, (ROWS_Y + SECOND_PAIRS) // 2, 2, TALL, features), BF16),
            pltpu.VMEM((4, features // 4, features), F32),
            dma((2, 12)),
        ],
        compiler_params=pltpu.CompilerParams(vmem_limit_bytes=VMEM_BYTES),
    )(hidden, d_feats, d_weight)


def solution(mesh):
    cols_x = mesh.shape["sub"] // CORES
    return jax.shard_map(
        functools.partial(shards, cols_x),
        mesh=mesh,
        in_specs=(
            P("sub", "dom"),
            P(),
            P("dom", None),
            P("dom", None),
            P("dom", None, None, None),
            P("dom", None, None),
            P("dom", None),
            P(None, ("dom", "sub")),
        ),
        out_specs=(P(None, ("dom", "sub")), P("sub", "dom"), P()),
        check_vma=False,
    )
```

```python
import functools

import jax
import jax.numpy as jnp
from jax import lax
from jax.experimental import pallas as pl
from jax.experimental.pallas import tpu as pltpu
from jax.sharding import PartitionSpec as P

ROWS_Y = 8
CORES = 2
ONES = 16
TALL = 16
SECOND_PAIRS = 4
VMEM_BYTES = 60 * 1024 * 1024
F32 = jnp.float32
BF16 = jnp.bfloat16
FAR_FIRST = {4: (2, 1, 3, 0), 2: (1, 0)}


def offset_of(position):
    return (position // 2 + 1) * (1 - 2 * (position % 2))


def order_by(keys, attributes, key_count):
    size = keys.shape[1]
    row = lax.broadcasted_iota(jnp.int32, (size, size), 0)
    lane = lax.broadcasted_iota(jnp.int32, (size, size), 1)

    def column(values):
        spread = jnp.broadcast_to(values, (size, size))
        return jnp.sum(jnp.where(row == lane, spread, 0.0), axis=1, keepdims=True)

    keys_column = column(keys)
    same = jnp.broadcast_to(keys, (size, size)) == keys_column
    less = jnp.broadcast_to(keys, (size, size)) < keys_column
    earlier = same & (lane < row)
    rank = jnp.sum(jnp.where(less | earlier, 1.0, 0.0), axis=1, keepdims=True)
    keep = jnp.minimum(jnp.sum(jnp.where(earlier, 1.0, 0.0), axis=1, keepdims=True), 1.0)
    hit = jnp.where(rank == lane.astype(F32), 1.0, 0.0)

    def placed(values):
        return jnp.sum(hit * values, axis=0, keepdims=True)

    wanted = lax.broadcasted_iota(jnp.int32, (size, key_count), 1).astype(F32)
    last = jnp.sum(jnp.where(keys_column <= wanted, 1.0, 0.0), axis=0, keepdims=True) - 1.0
    present = jnp.sum(jnp.where(keys_column == wanted, 1.0, 0.0), axis=0, keepdims=True)
    index_column = lax.broadcasted_iota(jnp.int32, (size, 1), 0).astype(F32)
    return (
        [placed(index_column)]
        + [placed(column(values)) for values in attributes]
        + [placed(keep), jnp.maximum(last, 0.0), jnp.minimum(present, 1.0)]
    )


def plan_kernel(blocks, table_len, list_ref, count_ref, dst_ref, src_ref, out_ref):
    _, offsets, capacity = list_ref.shape
    slots = offsets * capacity
    dst = dst_ref[...].astype(F32)
    src = src_ref[...].astype(F32)
    lane = lax.broadcasted_iota(jnp.int32, (1, slots), 1)
    listed = jnp.zeros((1, slots), jnp.int32)
    live = jnp.zeros((1, slots), jnp.int32)
    for j in range(offsets):
        for k in range(capacity):
            here = lane == j * capacity + k
            listed = jnp.where(here, list_ref[0, j, k], listed)
            live = jnp.where(here & (k < count_ref[0, j]), 1, live)
    owner = jnp.where(live == 1, listed, blocks).astype(F32)
    rows = (
        order_by(dst, [src], blocks)
        + order_by(src, [dst], table_len)
        + [listed.astype(F32)]
        + order_by(owner, [], blocks)
    )
    out_ref[...] = jnp.zeros_like(out_ref)
    for index, values in enumerate(rows):
        out_ref[index : index + 1, : values.shape[1]] = values.astype(jnp.int32)


def kernel(
    cols_x,
    plan,
    feats,
    weight,
    mask,
    cot,
    hidden,
    d_feats,
    d_weight,
    table,
    mask_int,
    mask_half,
    sums,
    w,
    wt,
    cot_v,
    outgoing,
    incoming,
    agg,
    full,
    scales,
    hid,
    d_pre,
    d_agg,
    dw_out,
    dw_own,
    core_in,
    half_out,
    y1_in,
    z1_in,
    first,
    second,
    z2_out,
    z2_in,
    x2_out,
    x2_in,
    x3_all,
    y3_all,
    line,
    square,
    gathered,
    back,
    scaled,
    returning,
    returned,
    slot_sums,
    result,
    local_sem,
    tile_sem,
    perm_sem,
    ret_sem,
    a2a_sem,
    back_sem,
    core_sem,
    y1_sem,
    z1_sem,
    x2_sem,
    z2_sem,
    x3_sem,
    y3_sem,
    x4_sem,
    z4_sem,
    y5_sem,
    z5_sem,
    x6_sem,
    gc_sem,
):
    width, span = feats.shape
    edges, block, _ = mask.shape
    features = weight.shape[0]
    blocks = span // block
    slots = returned.shape[0]
    offsets = perm_sem.shape[1]
    capacity = slots // offsets
    subs = cols_x * CORES
    per_sub = blocks // subs
    half = features // CORES
    doms = lax.axis_size("dom")
    deep = doms // ROWS_Y
    wide = features // 2
    row_z, across_z = deep // 2, deep // 4
    lanes = features // row_z

    dom, sub = lax.axis_index("dom"), lax.axis_index("sub")
    z, y = dom // ROWS_Y, dom % ROWS_Y
    x, core = sub // CORES, sub % CORES
    sibling = x * CORES + 1 - core

    def tile(index):
        return pl.ds(pl.multiple_of(index * block, block), block)

    def push(src, dst, sems, index, to_dom, to_sub):
        copy = pltpu.make_async_remote_copy(
            src_ref=src,
            dst_ref=dst,
            send_sem=sems.at[0, index],
            recv_sem=sems.at[1, index],
            device_id=(to_dom, to_sub),
            device_id_type=pl.DeviceIdType.MESH,
        )
        copy.start()
        return copy

    def fetch(src, dst, index):
        copy = pltpu.make_async_copy(src, dst, local_sem.at[index])
        copy.start()
        return copy

    in_dom = [lax.rem(dom + offset_of(j) + doms, doms) for j in range(offsets)]
    against = [lax.rem(dom - offset_of(j) + doms, doms) for j in range(offsets)]
    in_sub = [
        (o * CORES + d, lax.rem(x + o, cols_x) * CORES + lax.rem(core + d, CORES))
        for o in FAR_FIRST[cols_x]
        for d in range(CORES)
        if o or d
    ]
    in_x = [(o, lax.rem(x + o, cols_x)) for o in FAR_FIRST[cols_x] if o]
    in_z = [(o, lax.rem(z + o, deep)) for o in range(1, deep)]
    in_y = [(o, lax.rem(y + o, ROWS_Y)) for o in range(1, ROWS_Y)]

    def own_tile(b):
        return pltpu.make_async_copy(feats.at[:, tile(b)], table.at[b, :width], tile_sem.at[b])

    def start_tile(b, carry):
        own_tile(b).start()
        return carry

    lax.fori_loop(0, blocks, start_tile, 0)

    barrier = pltpu.get_barrier_semaphore()
    partners = (
        [(d, sub) for d in in_dom]
        + [(dom, s) for _, s in in_sub]
        + [(other * ROWS_Y + y, sub) for _, other in in_z]
        + [(z * ROWS_Y + other, sub) for _, other in in_y]
    )
    for partner in partners:
        pl.semaphore_signal(
            barrier, inc=1, device_id=partner, device_id_type=pl.DeviceIdType.MESH
        )

    quarter = edges // 4
    mask_in = [
        fetch(mask.at[pl.ds(i * quarter, quarter)], mask_int.at[pl.ds(i * quarter, quarter)], 1 + i)
        for i in range(4)
    ]
    w_in = fetch(weight, w, 5)
    cot_in = fetch(cot, cot_v, 6)

    def ones_below(t, carry):
        table[t, width:, :] = jnp.ones((ONES, block), BF16)
        return carry

    lax.fori_loop(0, blocks + slots, ones_below, 0)

    def wait_tile(b, carry):
        own_tile(b).wait()
        return carry

    lax.fori_loop(0, blocks, wait_tile, 0)
    for slot in range(slots):
        outgoing[slot] = table[plan[10, slot]][:width]
    pl.semaphore_wait(barrier, len(partners))

    sent = [
        push(
            outgoing.at[pl.ds(j * capacity, capacity)],
            incoming.at[pl.ds(j * capacity, capacity)],
            perm_sem,
            j,
            in_dom[j],
            sub,
        )
        for j in range(offsets)
    ]
    for i in range(4):
        mask_in[i].wait()

        def halve(e, carry):
            mask_half[e] = mask_int[e].astype(F32).astype(BF16)
            return carry

        lax.fori_loop(i * quarter, (i + 1) * quarter, halve, 0, unroll=2)
    for copy in sent:
        copy.wait_recv()
    table[blocks:, :width, :] = incoming[...]

    def forward(q, running):
        product = lax.dot_general(
            table[plan[1, q]],
            mask_half[plan[0, q]],
            (((1,), (1,)), ((), ())),
            preferred_element_type=F32,
        )
        running = running * plan[2, q].astype(F32) + product
        sums[q] = running
        return running

    lax.fori_loop(0, edges, forward, jnp.zeros((width + ONES, block), F32), unroll=4)

    def aggregate(s):
        def one(i, carry):
            b = s * per_sub + i
            total = sums[plan[3, b]] * plan[4, b].astype(F32)
            scale = lax.rsqrt(1.0 + total[width : width + 1])
            scales[b] = jnp.broadcast_to(scale, (8, block))
            own = table[b, :width, :].astype(F32)
            agg[s, :, tile(i)] = ((own + total[:width]) * scale).astype(BF16)
            return carry

        lax.fori_loop(0, per_sub, one, 0)

    own_rows = pl.ds(pl.multiple_of(sub * width, width), width)
    across = []
    for index, s in in_sub:
        aggregate(s)
        across.append(push(agg.at[s], full.at[own_rows], a2a_sem, index, dom, s))
    aggregate(sub)
    full[own_rows, :] = agg[sub]
    w_in.wait()
    strip = features // 4
    for i in range(4):
        wt[:, i * strip : (i + 1) * strip] = w[i * strip : (i + 1) * strip, :].T
    cot_in.wait()
    for copy in across:
        copy.wait_recv()

    def half_rows(i):
        return pl.ds(pl.multiple_of(i * half, half), half)

    def transform(i):
        rows = half_rows(i)
        pre = jnp.dot(w[rows, :], full[...], preferred_element_type=F32)
        gate = 1.0 / (1.0 + jnp.exp(-pre))
        hid[rows, :] = (pre * gate).astype(BF16)
        d_pre[rows, :] = (
            cot_v[rows, :].astype(F32) * gate * (1.0 + pre * (1.0 - gate))
        ).astype(BF16)

    def term(i):
        return lax.dot_general(
            d_pre[half_rows(i), :],
            full[...],
            (((1,), (1,)), ((), ())),
            preferred_element_type=F32,
        )

    transform(1 - core)
    dw_out[...] = term(1 - core).astype(BF16)
    to_core = push(dw_out, core_in, core_sem, 0, dom, sibling)
    transform(core)
    hid_out = fetch(hid, hidden, 7)

    def gradient(i, carry):
        rows = half_rows(i)
        product = jnp.dot(wt[rows, :], d_pre[...], preferred_element_type=F32).astype(BF16)
        for k in range(per_sub):
            d_agg[k, rows, :] = product[:, k * block : (k + 1) * block]
        return carry

    lax.fori_loop(0, CORES, gradient, 0)
    own_blocks = pl.ds(sub * per_sub, per_sub)
    backward = [
        push(
            d_agg.at[:, pl.ds(pl.multiple_of(s * width, width), width)],
            back.at[own_blocks],
            back_sem,
            index,
            dom,
            s,
        )
        for index, s in in_sub
    ]
    back[own_blocks] = d_agg[:, own_rows, :]
    dw_own[...] = term(core)
    to_core.wait_recv()

    def add_core(i, carry):
        rows = pl.ds(pl.multiple_of(i * 2 * TALL, 2 * TALL), 2 * TALL)
        total = dw_own[rows, :] + core_in[rows, :].astype(F32)
        dw_own[rows, :] = total
        half_out[rows, :] = total.astype(BF16)
        return carry

    lax.fori_loop(0, half // (2 * TALL), add_core, 0)

    def first_part(i):
        return pl.ds(pl.multiple_of(i * 2 * TALL, 2 * TALL), 2 * TALL), slice(None)

    def second_part(i):
        return (
            pl.ds(pl.multiple_of(ROWS_Y * 2 * TALL + (i // across_z) * 2 * TALL, 2 * TALL), 2 * TALL),
            pl.ds(pl.multiple_of((i % across_z) * 2 * lanes, 2 * lanes), 2 * lanes),
        )

    def one_tile(i, in_row):
        return (
            i // in_row,
            slice(None),
            pl.ds(pl.multiple_of((i % in_row) * lanes, lanes), lanes),
        )

    def tall_tile(i, in_row):
        return (
            pl.ds(pl.multiple_of((i // in_row) * TALL, TALL), TALL),
            pl.ds(pl.multiple_of((i % in_row) * lanes, lanes), lanes),
        )

    def over_z(src_of, dst_of, sems):
        return [
            push(src_of(other), dst_of(o), sems, o, other * ROWS_Y + y, sub) for o, other in in_z
        ]

    def over_y(src_of, dst_of, sems):
        return [
            push(src_of(other), dst_of(o), sems, o, z * ROWS_Y + other, sub) for o, other in in_y
        ]

    def over_x(src_of, dst_of, sems):
        return [
            push(src_of(other), dst_of(o), sems, o, dom, other * CORES + core)
            for o, other in in_x
        ]

    def arrive(copies):
        for copy in copies:
            copy.wait_recv()

    y1 = over_y(lambda i: half_out.at[first_part(i)], lambda o: y1_in.at[o - 1], y1_sem)
    z1 = over_z(lambda i: half_out.at[second_part(i)], lambda o: z1_in.at[o - 1], z1_sem)
    arrive(z1)
    total = dw_own[second_part(z)]
    for o in range(deep - 1):
        total = total + z1_in[o].astype(F32)
    second[...] = total
    for i in range(2):
        x2_out[i] = total[i * TALL : (i + 1) * TALL].astype(BF16)
    x2 = over_x(lambda i: x2_out.at[one_tile(i, 2)], lambda o: x2_in.at[o - 1], x2_sem)
    arrive(y1)
    total = dw_own[first_part(y)]
    for o in range(ROWS_Y - 1):
        total = total + y1_in[o].astype(F32)
    first[...] = total
    for i in range(2):
        z2_out[i] = total[i * TALL : (i + 1) * TALL].astype(BF16)
    z2 = over_z(lambda i: z2_out.at[one_tile(i, row_z)], lambda o: z2_in.at[o - 1], z2_sem)
    arrive(backward)

    def rescale(b, carry):
        scaled[b] = (back[b].astype(F32) * scales[b][:1]).astype(BF16)
        return carry

    lax.fori_loop(0, blocks, rescale, 0, unroll=2)

    def backward_edge(q, running):
        product = jnp.dot(scaled[plan[6, q]], mask_half[plan[5, q]], preferred_element_type=F32)
        running = running * plan[7, q].astype(F32) + product
        sums[q, :width, :] = running
        return running

    def some_edges(i, running):
        return lax.fori_loop(
            i * edges // 4, (i + 1) * edges // 4, backward_edge, running, unroll=4
        )

    running = some_edges(0, jnp.zeros((width, block), F32))
    arrive(x2)
    total = second[tall_tile(x, 2)]
    for o in range(cols_x - 1):
        total = total + x2_in[o].astype(F32)
    y3_all[y] = total.astype(BF16)
    y3 = over_y(lambda i: y3_all.at[y], lambda o: y3_all.at[y], y3_sem)
    arrive(z2)
    total = first[tall_tile(z, row_z)]
    for o in range(deep - 1):
        total = total + z2_in[o].astype(F32)
    x3_all[x] = total.astype(BF16)
    x3 = over_x(lambda i: x3_all.at[x], lambda o: x3_all.at[x], x3_sem)
    running = some_edges(1, running)
    running = some_edges(2, running)
    arrive(x3)
    total = x3_all[0].astype(F32)
    for other in range(1, cols_x):
        total = total + x3_all[other].astype(F32)
    mine = one_tile(z, row_z)
    line[mine] = total.astype(BF16)
    z4 = over_z(lambda i: line.at[mine], lambda o: line.at[mine], z4_sem)
    arrive(y3)
    total = y3_all[0].astype(F32)
    for other in range(1, ROWS_Y):
        total = total + y3_all[other].astype(F32)
    own_tile_x = one_tile(x, 2)
    square[own_tile_x] = total.astype(BF16)
    x4 = over_x(lambda i: square.at[own_tile_x], lambda o: square.at[own_tile_x], x4_sem)
    some_edges(3, running)
    home = []
    for j in range(offsets):
        for k in range(capacity):
            t = blocks + j * capacity + k
            returning[j * capacity + k] = (
                sums[plan[8, t]][:width] * plan[9, t].astype(F32)
            ).astype(BF16)
        home.append(
            push(
                returning.at[pl.ds(j * capacity, capacity)],
                returned.at[pl.ds(j * capacity, capacity)],
                ret_sem,
                j,
                against[j],
                sub,
            )
        )
    quarter_of = [
        (i // 2, slice(None), pl.ds(pl.multiple_of((i % 2) * wide, wide), wide))
        for i in (x, *(lax.rem(x - o + cols_x, cols_x) for o, _ in in_x))
    ]
    arrive(x4)
    square_at = (
        ROWS_Y + z // across_z,
        slice(None),
        slice(None),
        pl.ds(pl.multiple_of((z % across_z) * 2 * lanes, 2 * lanes), 2 * lanes),
    )
    gathered[square_at] = square[...]
    z5 = over_z(lambda i: square, lambda o: gathered.at[square_at], z5_sem)
    arrive(z4)
    own_quarter = quarter_of[0]
    gathered[(y,) + own_quarter] = line[own_quarter]
    y5 = over_y(
        lambda i: line.at[own_quarter],
        lambda o: gathered.at[(y,) + own_quarter],
        y5_sem,
    )

    def all_y(quarter):
        return gathered.at[(pl.ds(0, ROWS_Y),) + quarter]

    def to_results(src, at, index):
        own_parts.append(fetch(src, d_weight.at[(core,) + at], index))
        to_sibling.append(push(src, d_weight.at[(core,) + at], gc_sem, index, dom, sibling))

    own_parts = []
    to_sibling = []

    arrive(y5)
    x6 = over_x(lambda i: all_y(own_quarter), lambda o: all_y(own_quarter), x6_sem)
    to_results(all_y(own_quarter), (pl.ds(0, ROWS_Y),) + own_quarter, 0)
    arrive(home)

    def add_slot(i, running):
        running = running * plan[12, i].astype(F32) + returned[plan[11, i]].astype(F32)
        slot_sums[i] = running
        return running

    lax.fori_loop(0, slots, add_slot, jnp.zeros((width, block), F32))

    def finish(b, carry):
        result[:, tile(b)] = (
            scaled[b].astype(F32)
            + sums[plan[8, b]][:width] * plan[9, b].astype(F32)
            + slot_sums[plan[13, b]] * plan[14, b].astype(F32)
        ).astype(BF16)
        return carry

    lax.fori_loop(0, blocks, finish, 0, unroll=2)
    d_feats_out = fetch(result, d_feats, 8)
    arrive(z5)
    last_rows = (pl.ds(ROWS_Y, SECOND_PAIRS),)
    to_results(gathered.at[last_rows], last_rows, cols_x)
    for (o, _), copy, quarter in zip(in_x, x6, quarter_of[1:]):
        copy.wait_recv()
        to_results(all_y(quarter), (pl.ds(0, ROWS_Y),) + quarter, o)
    arrive(to_sibling)
    for copies in (
        sent, across, [to_core], backward, y1, z1, x2, z2, x3, y3, home, x4, z4, y5, z5, x6, to_sibling
    ):
        for copy in copies:
            copy.wait_send()
    hid_out.wait()
    d_feats_out.wait()
    for copy in own_parts:
        copy.wait()


def write_kernel(
    hid, d_feats, d_weight, hid_out, d_feats_out, d_weight_out, hid_v, d_feats_v, narrow, wide, sem
):
    parts, pairs, _, _, features = narrow.shape
    per_core = d_weight.shape[1] // pairs
    rows = features // parts
    columns = d_feats_v.shape[2]
    out_of = []
    into = []
    for i in range(parts):
        span, lanes = pl.ds(i * rows, rows), pl.ds(i * columns, columns)
        steps = (
            (
                d_weight.at[i // per_core, pl.ds((i % per_core) * pairs, pairs)],
                narrow.at[i],
                wide.at[i],
                d_weight_out.at[span],
            ),
            (hid.at[span], hid_v.at[i], hid_v.at[i], hid_out.at[span]),
            (d_feats.at[:, lanes], d_feats_v.at[i], d_feats_v.at[i], d_feats_out.at[:, lanes]),
        )
        for j, (here, arrive, leave, there) in enumerate(steps):
            into.append(pltpu.make_async_copy(here, arrive, sem.at[0, 3 * i + j]))
            out_of.append(pltpu.make_async_copy(leave, there, sem.at[1, 3 * i + j]))
    for copy in into:
        copy.start()
    for i in range(parts):
        for j in range(3):
            into[3 * i + j].wait()
            if j == 0:
                wide[i] = narrow[i].astype(F32).reshape(rows, features)
            out_of[3 * i + j].start()
    for copy in out_of:
        copy.wait()


def shards(cols_x, feats, weight, edge_dst, edge_src, edge_mask, send_list, send_count, cotangent):
    width, span = feats.shape
    _, edges, block, _ = edge_mask.shape
    features = weight.shape[0]
    blocks = span // block
    _, offsets, capacity = send_list.shape
    slots = offsets * capacity
    table_len = blocks + slots
    subs = cols_x * CORES
    labels = span // subs
    half = features // CORES
    deep = lax.axis_size("dom") // ROWS_Y
    lanes = features // (deep // 2)
    gather_shape = (CORES, ROWS_Y + SECOND_PAIRS, 2, TALL, features)
    vmem, smem, hbm, anywhere = (
        pl.BlockSpec(memory_space=space) for space in (pltpu.VMEM, pltpu.SMEM, pltpu.HBM, pl.ANY)
    )
    plan = pl.pallas_call(
        functools.partial(plan_kernel, blocks, table_len),
        out_shape=jax.ShapeDtypeStruct((16, 128), jnp.int32),
        in_specs=[smem, smem, vmem, vmem],
        out_specs=vmem,
        compiler_params=pltpu.CompilerParams(vmem_limit_bytes=VMEM_BYTES),
    )(send_list, send_count, edge_dst, edge_src)
    dma = pltpu.SemaphoreType.DMA
    hidden, d_feats, d_weight = pl.pallas_call(
        functools.partial(kernel, cols_x),
        out_shape=(
            jax.ShapeDtypeStruct((features, labels), BF16),
            jax.ShapeDtypeStruct((width, span), BF16),
            jax.ShapeDtypeStruct(gather_shape, BF16),
        ),
        in_specs=[smem] + [hbm] * 4,
        out_specs=(anywhere,) * 3,
        scratch_shapes=[
            pltpu.VMEM((table_len, width + ONES, block), BF16),
            pltpu.VMEM((edges, block, block), jnp.int32),
            pltpu.VMEM((edges, block, block), BF16),
            pltpu.VMEM((edges, width + ONES, block), F32),
            pltpu.VMEM((features, features), BF16),
            pltpu.VMEM((features, features), BF16),
            pltpu.VMEM((features, labels), BF16),
            pltpu.VMEM((slots, width, block), BF16),
            pltpu.VMEM((slots, width, block), BF16),
            pltpu.VMEM((subs, width, labels), BF16),
            pltpu.VMEM((features, labels), BF16),
            pltpu.VMEM((blocks, 8, block), F32),
            pltpu.VMEM((features, labels), BF16),
            pltpu.VMEM((features, labels), BF16),
            pltpu.VMEM((labels // block, features, block), BF16),
            pltpu.VMEM((half, features), BF16),
            pltpu.VMEM((half, features), F32),
            pltpu.VMEM((half, features), BF16),
            pltpu.VMEM((half, features), BF16),
            pltpu.VMEM((ROWS_Y - 1, 2 * TALL, features), BF16),
            pltpu.VMEM((deep - 1, 2 * TALL, 2 * lanes), BF16),
            pltpu.VMEM((2 * TALL, features), F32),
            pltpu.VMEM((2 * TALL, 2 * lanes), F32),
            pltpu.VMEM((2, TALL, features), BF16),
            pltpu.VMEM((deep - 1, TALL, lanes), BF16),
            pltpu.VMEM((2, TALL, 2 * lanes), BF16),
            pltpu.VMEM((cols_x - 1, TALL, lanes), BF16),
            pltpu.VMEM((cols_x, TALL, lanes), BF16),
            pltpu.VMEM((ROWS_Y, TALL, lanes), BF16),
            pltpu.VMEM((2, TALL, features), BF16),
            pltpu.VMEM((2, TALL, 2 * lanes), BF16),
            pltpu.VMEM(gather_shape[1:], BF16),
            pltpu.VMEM((blocks, width, block), BF16),
            pltpu.VMEM((blocks, width, block), BF16),
            pltpu.VMEM((slots, width, block), BF16),
            pltpu.VMEM((slots, width, block), BF16),
            pltpu.VMEM((slots, width, block), F32),
            pltpu.VMEM((width, span), BF16),
            dma((10,)),
            dma((blocks,)),
            dma((2, offsets)),
            dma((2, offsets)),
            dma((2, subs)),
            dma((2, subs)),
            dma((2, 1)),
            dma((2, ROWS_Y)),
            dma((2, deep)),
            dma((2, cols_x)),
            dma((2, deep)),
            dma((2, cols_x)),
            dma((2, ROWS_Y)),
            dma((2, cols_x)),
            dma((2, deep)),
            dma((2, ROWS_Y)),
            dma((2, deep)),
            dma((2, cols_x)),
            dma((2, cols_x + 1)),
        ],
        compiler_params=pltpu.CompilerParams(
            collective_id=0, has_side_effects=True, vmem_limit_bytes=VMEM_BYTES
        ),
    )(plan, feats, weight, edge_mask[0], cotangent)
    return pl.pallas_call(
        write_kernel,
        out_shape=(
            jax.ShapeDtypeStruct((features, labels), BF16),
            jax.ShapeDtypeStruct((width, span), BF16),
            jax.ShapeDtypeStruct((features, features), F32),
        ),
        in_specs=[anywhere] * 3,
        out_specs=(hbm,) * 3,
        scratch_shapes=[
            pltpu.VMEM((4, features // 4, labels), BF16),
            pltpu.VMEM((4, width, span // 4), BF16),
            pltpu.VMEM((4, (ROWS_Y + SECOND_PAIRS) // 2, 2, TALL, features), BF16),
            pltpu.VMEM((4, features // 4, features), F32),
            dma((2, 12)),
        ],
        compiler_params=pltpu.CompilerParams(vmem_limit_bytes=VMEM_BYTES),
    )(hidden, d_feats, d_weight)


def solution(mesh):
    cols_x = mesh.shape["sub"] // CORES
    return jax.shard_map(
        functools.partial(shards, cols_x),
        mesh=mesh,
        in_specs=(
            P("sub", "dom"),
            P(),
            P("dom", None),
            P("dom", None),
            P("dom", None, None, None),
            P("dom", None, None),
            P("dom", None),
            P(None, ("dom", "sub")),
        ),
        out_specs=(P(None, ("dom", "sub")), P("sub", "dom"), P()),
        check_vma=False,
    )
```

```python
import functools

import jax
import jax.numpy as jnp
from jax import lax
from jax.experimental import pallas as pl
from jax.experimental.pallas import tpu as pltpu
from jax.sharding import PartitionSpec as P

ROWS_Y = 8
CORES = 2
ONES = 16
VMEM_BYTES = 60 * 1024 * 1024
F32 = jnp.float32
BF16 = jnp.bfloat16
FAR_FIRST = {4: (2, 1, 3, 0), 2: (1, 0)}


def offset_of(position):
    return (position // 2 + 1) * (1 - 2 * (position % 2))


def order_by(keys, attributes, key_count):
    size = keys.shape[1]
    row = lax.broadcasted_iota(jnp.int32, (size, size), 0)
    lane = lax.broadcasted_iota(jnp.int32, (size, size), 1)

    def column(values):
        spread = jnp.broadcast_to(values, (size, size))
        return jnp.sum(jnp.where(row == lane, spread, 0.0), axis=1, keepdims=True)

    keys_column = column(keys)
    same = jnp.broadcast_to(keys, (size, size)) == keys_column
    less = jnp.broadcast_to(keys, (size, size)) < keys_column
    earlier = same & (lane < row)
    rank = jnp.sum(jnp.where(less | earlier, 1.0, 0.0), axis=1, keepdims=True)
    keep = jnp.minimum(jnp.sum(jnp.where(earlier, 1.0, 0.0), axis=1, keepdims=True), 1.0)
    hit = jnp.where(rank == lane.astype(F32), 1.0, 0.0)

    def placed(values):
        return jnp.sum(hit * values, axis=0, keepdims=True)

    wanted = lax.broadcasted_iota(jnp.int32, (size, key_count), 1).astype(F32)
    last = jnp.sum(jnp.where(keys_column <= wanted, 1.0, 0.0), axis=0, keepdims=True) - 1.0
    present = jnp.sum(jnp.where(keys_column == wanted, 1.0, 0.0), axis=0, keepdims=True)
    index_column = lax.broadcasted_iota(jnp.int32, (size, 1), 0).astype(F32)
    return (
        [placed(index_column)]
        + [placed(column(values)) for values in attributes]
        + [placed(keep), jnp.maximum(last, 0.0), jnp.minimum(present, 1.0)]
    )


def plan_kernel(blocks, table_len, list_ref, count_ref, dst_ref, src_ref, out_ref):
    _, offsets, capacity = list_ref.shape
    slots = offsets * capacity
    dst = dst_ref[...].astype(F32)
    src = src_ref[...].astype(F32)
    lane = lax.broadcasted_iota(jnp.int32, (1, slots), 1)
    listed = jnp.zeros((1, slots), jnp.int32)
    live = jnp.zeros((1, slots), jnp.int32)
    for j in range(offsets):
        for k in range(capacity):
            here = lane == j * capacity + k
            listed = jnp.where(here, list_ref[0, j, k], listed)
            live = jnp.where(here & (k < count_ref[0, j]), 1, live)
    owner = jnp.where(live == 1, listed, blocks).astype(F32)
    rows = (
        order_by(dst, [src], blocks)
        + order_by(src, [dst], table_len)
        + [listed.astype(F32)]
        + order_by(owner, [], blocks)
    )
    out_ref[...] = jnp.zeros_like(out_ref)
    for index, values in enumerate(rows):
        out_ref[index : index + 1, : values.shape[1]] = values.astype(jnp.int32)


def kernel(
    cols_x,
    plan,
    feats,
    weight,
    mask,
    cot,
    hidden,
    d_feats,
    d_weight,
    table,
    mask_int,
    mask_half,
    sums,
    w,
    wt,
    cot_v,
    outgoing,
    incoming,
    agg,
    full,
    scales,
    hid,
    d_pre,
    d_agg,
    dw_out,
    dw_own,
    core_in,
    x_out,
    x_in,
    z_out,
    z_in,
    y_all,
    summed,
    gathered,
    back,
    scaled,
    returning,
    returned,
    slot_sums,
    result,
    local_sem,
    tile_sem,
    perm_sem,
    ret_sem,
    a2a_sem,
    back_sem,
    core_sem,
    x_sem,
    z_sem,
    y_sem,
    gz_sem,
    gx_sem,
    gc_sem,
):
    width, span = feats.shape
    edges, block, _ = mask.shape
    features = weight.shape[0]
    blocks = span // block
    slots = returned.shape[0]
    offsets = perm_sem.shape[1]
    capacity = slots // offsets
    subs = cols_x * CORES
    per_sub = blocks // subs
    half = features // CORES
    xrows = half // cols_x
    doms = lax.axis_size("dom")
    deep = doms // ROWS_Y
    wide = features // 2

    dom, sub = lax.axis_index("dom"), lax.axis_index("sub")
    z, y = dom // ROWS_Y, dom % ROWS_Y
    x, core = sub // CORES, sub % CORES
    sibling = x * CORES + 1 - core

    def tile(index):
        return pl.ds(pl.multiple_of(index * block, block), block)

    def push(src, dst, sems, index, to_dom, to_sub):
        copy = pltpu.make_async_remote_copy(
            src_ref=src,
            dst_ref=dst,
            send_sem=sems.at[0, index],
            recv_sem=sems.at[1, index],
            device_id=(to_dom, to_sub),
            device_id_type=pl.DeviceIdType.MESH,
        )
        copy.start()
        return copy

    def fetch(src, dst, index):
        copy = pltpu.make_async_copy(src, dst, local_sem.at[index])
        copy.start()
        return copy

    in_dom = [lax.rem(dom + offset_of(j) + doms, doms) for j in range(offsets)]
    against = [lax.rem(dom - offset_of(j) + doms, doms) for j in range(offsets)]
    in_sub = [
        (o * CORES + d, lax.rem(x + o, cols_x) * CORES + lax.rem(core + d, CORES))
        for o in FAR_FIRST[cols_x]
        for d in range(CORES)
        if o or d
    ]
    in_x = [(o, lax.rem(x + o, cols_x)) for o in FAR_FIRST[cols_x] if o]
    in_z = [(o, lax.rem(z + o, deep)) for o in range(1, deep)]
    in_y = [(o, lax.rem(y + o, ROWS_Y)) for o in range(1, ROWS_Y)]

    def own_tile(b):
        return pltpu.make_async_copy(feats.at[:, tile(b)], table.at[b, :width], tile_sem.at[b])

    def start_tile(b, carry):
        own_tile(b).start()
        return carry

    lax.fori_loop(0, blocks, start_tile, 0)

    barrier = pltpu.get_barrier_semaphore()
    partners = (
        [(d, sub) for d in in_dom]
        + [(dom, s) for _, s in in_sub]
        + [(other * ROWS_Y + y, sub) for _, other in in_z]
        + [(z * ROWS_Y + other, sub) for _, other in in_y]
    )
    for partner in partners:
        pl.semaphore_signal(
            barrier, inc=1, device_id=partner, device_id_type=pl.DeviceIdType.MESH
        )

    quarter = edges // 4
    mask_in = [
        fetch(mask.at[pl.ds(i * quarter, quarter)], mask_int.at[pl.ds(i * quarter, quarter)], 1 + i)
        for i in range(4)
    ]
    w_in = fetch(weight, w, 5)
    cot_in = fetch(cot, cot_v, 6)

    def ones_below(t, carry):
        table[t, width:, :] = jnp.ones((ONES, block), BF16)
        return carry

    lax.fori_loop(0, blocks + slots, ones_below, 0)

    def wait_tile(b, carry):
        own_tile(b).wait()
        return carry

    lax.fori_loop(0, blocks, wait_tile, 0)
    for slot in range(slots):
        outgoing[slot] = table[plan[10, slot]][:width]
    pl.semaphore_wait(barrier, len(partners))

    sent = [
        push(
            outgoing.at[pl.ds(j * capacity, capacity)],
            incoming.at[pl.ds(j * capacity, capacity)],
            perm_sem,
            j,
            in_dom[j],
            sub,
        )
        for j in range(offsets)
    ]
    for i in range(4):
        mask_in[i].wait()

        def halve(e, carry):
            mask_half[e] = mask_int[e].astype(F32).astype(BF16)
            return carry

        lax.fori_loop(i * quarter, (i + 1) * quarter, halve, 0, unroll=2)
    for copy in sent:
        copy.wait_recv()
    table[blocks:, :width, :] = incoming[...]

    def forward(q, running):
        product = lax.dot_general(
            table[plan[1, q]],
            mask_half[plan[0, q]],
            (((1,), (1,)), ((), ())),
            preferred_element_type=F32,
        )
        running = running * plan[2, q].astype(F32) + product
        sums[q] = running
        return running

    lax.fori_loop(0, edges, forward, jnp.zeros((width + ONES, block), F32), unroll=4)

    def aggregate(s):
        def one(i, carry):
            b = s * per_sub + i
            total = sums[plan[3, b]] * plan[4, b].astype(F32)
            scale = lax.rsqrt(1.0 + total[width : width + 1])
            scales[b] = jnp.broadcast_to(scale, (8, block))
            own = table[b, :width, :].astype(F32)
            agg[s, :, tile(i)] = ((own + total[:width]) * scale).astype(BF16)
            return carry

        lax.fori_loop(0, per_sub, one, 0)

    own_rows = pl.ds(pl.multiple_of(sub * width, width), width)
    across = []
    for index, s in in_sub:
        aggregate(s)
        across.append(push(agg.at[s], full.at[own_rows], a2a_sem, index, dom, s))
    aggregate(sub)
    full[own_rows, :] = agg[sub]
    w_in.wait()
    strip = features // 4
    for i in range(4):
        wt[:, i * strip : (i + 1) * strip] = w[i * strip : (i + 1) * strip, :].T
    cot_in.wait()
    for copy in across:
        copy.wait_recv()

    def half_rows(i):
        return pl.ds(pl.multiple_of(i * half, half), half)

    def transform(i):
        rows = half_rows(i)
        pre = jnp.dot(w[rows, :], full[...], preferred_element_type=F32)
        gate = 1.0 / (1.0 + jnp.exp(-pre))
        hid[rows, :] = (pre * gate).astype(BF16)
        d_pre[rows, :] = (
            cot_v[rows, :].astype(F32) * gate * (1.0 + pre * (1.0 - gate))
        ).astype(BF16)

    def term(i):
        return lax.dot_general(
            d_pre[half_rows(i), :],
            full[...],
            (((1,), (1,)), ((), ())),
            preferred_element_type=F32,
        )

    transform(1 - core)
    dw_out[...] = term(1 - core).astype(BF16)
    to_core = push(dw_out, core_in, core_sem, 0, dom, sibling)
    transform(core)
    hid_out = fetch(hid, hidden, 7)
    dw_own[...] = term(core)

    def x_rows(i):
        return pl.ds(pl.multiple_of(i * xrows, xrows), xrows)

    to_core.wait_recv()

    def add_core(i, carry):
        total = dw_own[x_rows(i), :] + core_in[x_rows(i), :].astype(F32)
        dw_own[x_rows(i), :] = total
        x_out[x_rows(i), :] = total.astype(BF16)
        return carry

    lax.fori_loop(0, cols_x, add_core, 0)
    to_x = [
        push(x_out.at[x_rows(other)], x_in.at[o - 1], x_sem, o, dom, other * CORES + core)
        for o, other in in_x
    ]

    def gradient(i, carry):
        rows = half_rows(i)
        product = jnp.dot(wt[rows, :], d_pre[...], preferred_element_type=F32).astype(BF16)
        for k in range(per_sub):
            d_agg[k, rows, :] = product[:, k * block : (k + 1) * block]
        return carry

    lax.fori_loop(0, CORES, gradient, 0)

    def z_part(i):
        return (
            pl.ds(pl.multiple_of((i // 2) * 16, 16), 16),
            pl.ds(pl.multiple_of((i % 2) * wide, wide), wide),
        )

    for copy in to_x:
        copy.wait_recv()
    total = dw_own[x_rows(x), :]
    for o in range(cols_x - 1):
        total = total + x_in[o].astype(F32)
    dw_own[:xrows, :] = total
    z_out[...] = total.astype(BF16)
    to_z = [
        push(z_out.at[z_part(other)], z_in.at[o - 1], z_sem, o, other * ROWS_Y + y, sub)
        for o, other in in_z
    ]
    own_blocks = pl.ds(sub * per_sub, per_sub)
    backward = [
        push(
            d_agg.at[:, pl.ds(pl.multiple_of(s * width, width), width)],
            back.at[own_blocks],
            back_sem,
            index,
            dom,
            s,
        )
        for index, s in in_sub
    ]
    back[own_blocks] = d_agg[:, own_rows, :]
    for copy in to_z:
        copy.wait_recv()
    rows, columns = z_part(z)
    total = dw_own[rows, columns]
    for o in range(deep - 1):
        total = total + z_in[o].astype(F32)
    y_all[y] = total.astype(BF16)
    to_y = [
        push(y_all.at[y], y_all.at[y], y_sem, o, z * ROWS_Y + other, sub) for o, other in in_y
    ]
    for copy in to_y:
        copy.wait_recv()
    total = y_all[0].astype(F32)
    for other in range(1, ROWS_Y):
        total = total + y_all[other].astype(F32)
    summed[...] = total.astype(BF16)

    def x_strip(of_core, of_x):
        return pl.ds(pl.multiple_of(of_core * half + of_x * xrows, xrows), xrows)

    mine = (
        pl.ds(pl.multiple_of(core * half + x * xrows + (z // 2) * 16, 16), 16),
        pl.ds(pl.multiple_of((z % 2) * wide, wide), wide),
    )
    over_z = [
        push(summed, gathered.at[mine], gz_sem, o, other * ROWS_Y + y, sub) for o, other in in_z
    ]
    gathered[mine] = summed[...]
    for copy in backward:
        copy.wait_recv()

    def rescale(b, carry):
        scaled[b] = (back[b].astype(F32) * scales[b][:1]).astype(BF16)
        return carry

    lax.fori_loop(0, blocks, rescale, 0, unroll=2)
    def backward_edge(q, running):
        product = jnp.dot(
            scaled[plan[6, q]], mask_half[plan[5, q]], preferred_element_type=F32
        )
        running = running * plan[7, q].astype(F32) + product
        sums[q, :width, :] = running
        return running

    lax.fori_loop(0, edges, backward_edge, jnp.zeros((width, block), F32), unroll=4)
    home = []
    for j in range(offsets):
        for k in range(capacity):
            t = blocks + j * capacity + k
            returning[j * capacity + k] = (
                sums[plan[8, t]][:width] * plan[9, t].astype(F32)
            ).astype(BF16)
        home.append(
            push(
                returning.at[pl.ds(j * capacity, capacity)],
                returned.at[pl.ds(j * capacity, capacity)],
                ret_sem,
                j,
                against[j],
                sub,
            )
        )
    for copy in over_z:
        copy.wait_recv()
    def to_results(of_x, index):
        rows = x_strip(core, of_x)
        own_parts.append(fetch(gathered.at[rows], d_weight.at[rows], index))
        over_core.append(
            push(gathered.at[rows], d_weight.at[rows], gc_sem, index, dom, sibling)
        )

    own_parts = []
    over_core = []
    strip_x = gathered.at[x_strip(core, x)]
    over_x = [
        push(strip_x, strip_x, gx_sem, o, dom, other * CORES + core) for o, other in in_x
    ]
    to_results(x, 0)
    for copy in home:
        copy.wait_recv()

    def add_slot(i, running):
        running = running * plan[12, i].astype(F32) + returned[plan[11, i]].astype(F32)
        slot_sums[i] = running
        return running

    lax.fori_loop(0, slots, add_slot, jnp.zeros((width, block), F32))

    def finish(b, carry):
        result[:, tile(b)] = (
            scaled[b].astype(F32)
            + sums[plan[8, b]][:width] * plan[9, b].astype(F32)
            + slot_sums[plan[13, b]] * plan[14, b].astype(F32)
        ).astype(BF16)
        return carry

    lax.fori_loop(0, blocks, finish, 0, unroll=2)
    d_feats_out = fetch(result, d_feats, 8)
    for (o, _), copy in zip(in_x, over_x):
        copy.wait_recv()
        to_results(lax.rem(x - o + cols_x, cols_x), o)
    for copy in over_core:
        copy.wait_recv()
    for copy in (
        sent
        + across
        + [to_core]
        + to_x
        + backward
        + to_z
        + to_y
        + home
        + over_z
        + over_x
        + over_core
    ):
        copy.wait_send()
    hid_out.wait()
    d_feats_out.wait()
    for copy in own_parts:
        copy.wait()


def write_kernel(
    hid, d_feats, d_weight, hid_out, d_feats_out, d_weight_out, hid_v, d_feats_v, narrow, wide, sem
):
    parts, rows, _ = narrow.shape
    columns = d_feats_v.shape[2]
    out_of = []
    into = []
    for i in range(parts):
        span, lanes = pl.ds(i * rows, rows), pl.ds(i * columns, columns)
        steps = (
            (d_weight.at[span], narrow.at[i], wide.at[i], d_weight_out.at[span]),
            (hid.at[span], hid_v.at[i], hid_v.at[i], hid_out.at[span]),
            (d_feats.at[:, lanes], d_feats_v.at[i], d_feats_v.at[i], d_feats_out.at[:, lanes]),
        )
        for j, (here, arrive, leave, there) in enumerate(steps):
            into.append(pltpu.make_async_copy(here, arrive, sem.at[0, 3 * i + j]))
            out_of.append(pltpu.make_async_copy(leave, there, sem.at[1, 3 * i + j]))
    for copy in into:
        copy.start()
    for i in range(parts):
        for j in range(3):
            into[3 * i + j].wait()
            if j == 0:
                wide[i] = narrow[i].astype(F32)
            out_of[3 * i + j].start()
    for copy in out_of:
        copy.wait()


def shards(cols_x, feats, weight, edge_dst, edge_src, edge_mask, send_list, send_count, cotangent):
    width, span = feats.shape
    _, edges, block, _ = edge_mask.shape
    features = weight.shape[0]
    blocks = span // block
    _, offsets, capacity = send_list.shape
    slots = offsets * capacity
    table_len = blocks + slots
    subs = cols_x * CORES
    labels = span // subs
    half = features // CORES
    xrows = half // cols_x
    deep = lax.axis_size("dom") // ROWS_Y
    vmem, smem, hbm, anywhere = (
        pl.BlockSpec(memory_space=space) for space in (pltpu.VMEM, pltpu.SMEM, pltpu.HBM, pl.ANY)
    )
    plan = pl.pallas_call(
        functools.partial(plan_kernel, blocks, table_len),
        out_shape=jax.ShapeDtypeStruct((16, 128), jnp.int32),
        in_specs=[smem, smem, vmem, vmem],
        out_specs=vmem,
        compiler_params=pltpu.CompilerParams(vmem_limit_bytes=VMEM_BYTES),
    )(send_list, send_count, edge_dst, edge_src)
    dma = pltpu.SemaphoreType.DMA
    hidden, d_feats, d_weight = pl.pallas_call(
        functools.partial(kernel, cols_x),
        out_shape=(
            jax.ShapeDtypeStruct((features, labels), BF16),
            jax.ShapeDtypeStruct((width, span), BF16),
            jax.ShapeDtypeStruct((features, features), BF16),
        ),
        in_specs=[smem] + [hbm] * 4,
        out_specs=(anywhere,) * 3,
        scratch_shapes=[
            pltpu.VMEM((table_len, width + ONES, block), BF16),
            pltpu.VMEM((edges, block, block), jnp.int32),
            pltpu.VMEM((edges, block, block), BF16),
            pltpu.VMEM((edges, width + ONES, block), F32),
            pltpu.VMEM((features, features), BF16),
            pltpu.VMEM((features, features), BF16),
            pltpu.VMEM((features, labels), BF16),
            pltpu.VMEM((slots, width, block), BF16),
            pltpu.VMEM((slots, width, block), BF16),
            pltpu.VMEM((subs, width, labels), BF16),
            pltpu.VMEM((features, labels), BF16),
            pltpu.VMEM((blocks, 8, block), F32),
            pltpu.VMEM((features, labels), BF16),
            pltpu.VMEM((features, labels), BF16),
            pltpu.VMEM((labels // block, features, block), BF16),
            pltpu.VMEM((half, features), BF16),
            pltpu.VMEM((half, features), F32),
            pltpu.VMEM((half, features), BF16),
            pltpu.VMEM((half, features), BF16),
            pltpu.VMEM((cols_x - 1, xrows, features), BF16),
            pltpu.VMEM((xrows, features), BF16),
            pltpu.VMEM((deep - 1, 16, features // 2), BF16),
            pltpu.VMEM((ROWS_Y, 16, features // 2), BF16),
            pltpu.VMEM((16, features // 2), BF16),
            pltpu.VMEM((features, features), BF16),
            pltpu.VMEM((blocks, width, block), BF16),
            pltpu.VMEM((blocks, width, block), BF16),
            pltpu.VMEM((slots, width, block), BF16),
            pltpu.VMEM((slots, width, block), BF16),
            pltpu.VMEM((slots, width, block), F32),
            pltpu.VMEM((width, span), BF16),
            dma((10,)),
            dma((blocks,)),
            dma((2, offsets)),
            dma((2, offsets)),
            dma((2, subs)),
            dma((2, subs)),
            dma((2, 1)),
            dma((2, cols_x)),
            dma((2, deep)),
            dma((2, ROWS_Y)),
            dma((2, deep)),
            dma((2, cols_x)),
            dma((2, cols_x)),
        ],
        compiler_params=pltpu.CompilerParams(
            collective_id=0, has_side_effects=True, vmem_limit_bytes=VMEM_BYTES
        ),
    )(plan, feats, weight, edge_mask[0], cotangent)
    return pl.pallas_call(
        write_kernel,
        out_shape=(
            jax.ShapeDtypeStruct((features, labels), BF16),
            jax.ShapeDtypeStruct((width, span), BF16),
            jax.ShapeDtypeStruct((features, features), F32),
        ),
        in_specs=[anywhere] * 3,
        out_specs=(hbm,) * 3,
        scratch_shapes=[
            pltpu.VMEM((4, features // 4, labels), BF16),
            pltpu.VMEM((4, width, span // 4), BF16),
            pltpu.VMEM((4, features // 4, features), BF16),
            pltpu.VMEM((4, features // 4, features), F32),
            dma((2, 12)),
        ],
        compiler_params=pltpu.CompilerParams(vmem_limit_bytes=VMEM_BYTES),
    )(hidden, d_feats, d_weight)


def solution(mesh):
    cols_x = mesh.shape["sub"] // CORES
    return jax.shard_map(
        functools.partial(shards, cols_x),
        mesh=mesh,
        in_specs=(
            P("sub", "dom"),
            P(),
            P("dom", None),
            P("dom", None),
            P("dom", None, None, None),
            P("dom", None, None),
            P("dom", None),
            P(None, ("dom", "sub")),
        ),
        out_specs=(P(None, ("dom", "sub")), P("sub", "dom"), P()),
        check_vma=False,
    )
```

```python
import functools

import jax
import jax.numpy as jnp
from jax import lax
from jax.experimental import pallas as pl
from jax.experimental.pallas import tpu as pltpu
from jax.sharding import PartitionSpec as P

ROWS_Y = 8
CORES = 2
ONES = 16
VMEM_BYTES = 60 * 1024 * 1024
F32 = jnp.float32
BF16 = jnp.bfloat16
FAR_FIRST = {4: (2, 1, 3, 0), 2: (1, 0)}


def offset_of(position):
    return (position // 2 + 1) * (1 - 2 * (position % 2))


def order_by(keys, attributes, key_count):
    size = keys.shape[1]
    row = lax.broadcasted_iota(jnp.int32, (size, size), 0)
    lane = lax.broadcasted_iota(jnp.int32, (size, size), 1)

    def column(values):
        spread = jnp.broadcast_to(values, (size, size))
        return jnp.sum(jnp.where(row == lane, spread, 0.0), axis=1, keepdims=True)

    keys_column = column(keys)
    same = jnp.broadcast_to(keys, (size, size)) == keys_column
    less = jnp.broadcast_to(keys, (size, size)) < keys_column
    earlier = same & (lane < row)
    rank = jnp.sum(jnp.where(less | earlier, 1.0, 0.0), axis=1, keepdims=True)
    keep = jnp.minimum(jnp.sum(jnp.where(earlier, 1.0, 0.0), axis=1, keepdims=True), 1.0)
    hit = jnp.where(rank == lane.astype(F32), 1.0, 0.0)

    def placed(values):
        return jnp.sum(hit * values, axis=0, keepdims=True)

    wanted = lax.broadcasted_iota(jnp.int32, (size, key_count), 1).astype(F32)
    last = jnp.sum(jnp.where(keys_column <= wanted, 1.0, 0.0), axis=0, keepdims=True) - 1.0
    present = jnp.sum(jnp.where(keys_column == wanted, 1.0, 0.0), axis=0, keepdims=True)
    index_column = lax.broadcasted_iota(jnp.int32, (size, 1), 0).astype(F32)
    return (
        [placed(index_column)]
        + [placed(column(values)) for values in attributes]
        + [placed(keep), jnp.maximum(last, 0.0), jnp.minimum(present, 1.0)]
    )


def plan_kernel(blocks, table_len, list_ref, count_ref, dst_ref, src_ref, out_ref):
    _, offsets, capacity = list_ref.shape
    slots = offsets * capacity
    dst = dst_ref[...].astype(F32)
    src = src_ref[...].astype(F32)
    lane = lax.broadcasted_iota(jnp.int32, (1, slots), 1)
    listed = jnp.zeros((1, slots), jnp.int32)
    live = jnp.zeros((1, slots), jnp.int32)
    for j in range(offsets):
        for k in range(capacity):
            here = lane == j * capacity + k
            listed = jnp.where(here, list_ref[0, j, k], listed)
            live = jnp.where(here & (k < count_ref[0, j]), 1, live)
    owner = jnp.where(live == 1, listed, blocks).astype(F32)
    rows = (
        order_by(dst, [src], blocks)
        + order_by(src, [dst], table_len)
        + [listed.astype(F32)]
        + order_by(owner, [], blocks)
    )
    out_ref[...] = jnp.zeros_like(out_ref)
    for index, values in enumerate(rows):
        out_ref[index : index + 1, : values.shape[1]] = values.astype(jnp.int32)


def kernel(
    cols_x,
    plan,
    feats,
    weight,
    mask,
    cot,
    hidden,
    d_feats,
    d_weight,
    table,
    mask_int,
    mask_half,
    sums,
    w,
    wt,
    cot_v,
    outgoing,
    incoming,
    agg,
    full,
    scales,
    hid,
    d_pre,
    d_agg,
    dw_out,
    dw_own,
    core_in,
    x_out,
    x_in,
    z_out,
    z_in,
    y_all,
    summed,
    gathered,
    back,
    scaled,
    returning,
    returned,
    slot_sums,
    base,
    result,
    local_sem,
    tile_sem,
    perm_sem,
    ret_sem,
    a2a_sem,
    back_sem,
    core_sem,
    x_sem,
    z_sem,
    y_sem,
    gz_sem,
    gx_sem,
    gc_sem,
):
    width, span = feats.shape
    edges, block, _ = mask.shape
    features = weight.shape[0]
    blocks = span // block
    slots = returned.shape[0]
    offsets = perm_sem.shape[1]
    capacity = slots // offsets
    subs = cols_x * CORES
    per_sub = blocks // subs
    half = features // CORES
    xrows = half // cols_x
    doms = lax.axis_size("dom")
    deep = doms // ROWS_Y
    wide = features // 2

    dom, sub = lax.axis_index("dom"), lax.axis_index("sub")
    z, y = dom // ROWS_Y, dom % ROWS_Y
    x, core = sub // CORES, sub % CORES
    sibling = x * CORES + 1 - core

    def tile(index):
        return pl.ds(pl.multiple_of(index * block, block), block)

    def push(src, dst, sems, index, to_dom, to_sub):
        copy = pltpu.make_async_remote_copy(
            src_ref=src,
            dst_ref=dst,
            send_sem=sems.at[0, index],
            recv_sem=sems.at[1, index],
            device_id=(to_dom, to_sub),
            device_id_type=pl.DeviceIdType.MESH,
        )
        copy.start()
        return copy

    def fetch(src, dst, index):
        copy = pltpu.make_async_copy(src, dst, local_sem.at[index])
        copy.start()
        return copy

    in_dom = [lax.rem(dom + offset_of(j) + doms, doms) for j in range(offsets)]
    against = [lax.rem(dom - offset_of(j) + doms, doms) for j in range(offsets)]
    in_sub = [
        (o * CORES + d, lax.rem(x + o, cols_x) * CORES + lax.rem(core + d, CORES))
        for o in FAR_FIRST[cols_x]
        for d in range(CORES)
        if o or d
    ]
    in_x = [(o, lax.rem(x + o, cols_x)) for o in FAR_FIRST[cols_x] if o]
    in_z = [(o, lax.rem(z + o, deep)) for o in range(1, deep)]
    in_y = [(o, lax.rem(y + o, ROWS_Y)) for o in range(1, ROWS_Y)]

    def own_tile(b):
        return pltpu.make_async_copy(feats.at[:, tile(b)], table.at[b, :width], tile_sem.at[b])

    def start_tile(b, carry):
        own_tile(b).start()
        return carry

    lax.fori_loop(0, blocks, start_tile, 0)

    barrier = pltpu.get_barrier_semaphore()
    partners = (
        [(d, sub) for d in in_dom]
        + [(dom, s) for _, s in in_sub]
        + [(other * ROWS_Y + y, sub) for _, other in in_z]
        + [(z * ROWS_Y + other, sub) for _, other in in_y]
    )
    for partner in partners:
        pl.semaphore_signal(
            barrier, inc=1, device_id=partner, device_id_type=pl.DeviceIdType.MESH
        )


    def ones_below(t, carry):
        table[t, width:, :] = jnp.ones((ONES, block), BF16)
        return carry

    lax.fori_loop(0, blocks + slots, ones_below, 0)

    def wait_tile(b, carry):
        own_tile(b).wait()
        return carry

    lax.fori_loop(0, blocks, wait_tile, 0)
    for slot in range(slots):
        outgoing[slot] = table[plan[10, slot]][:width]
    pl.semaphore_wait(barrier, len(partners))

    sent = [
        push(
            outgoing.at[pl.ds(j * capacity, capacity)],
            incoming.at[pl.ds(j * capacity, capacity)],
            perm_sem,
            j,
            in_dom[j],
            sub,
        )
        for j in reversed(range(offsets))
    ]
    quarter = edges // 4
    mask_in = [
        fetch(mask.at[pl.ds(i * quarter, quarter)], mask_int.at[pl.ds(i * quarter, quarter)], 1 + i)
        for i in range(4)
    ]
    w_in = fetch(weight, w, 5)
    cot_in = fetch(cot, cot_v, 6)
    for i in range(4):
        mask_in[i].wait()

        def halve(e, carry):
            mask_half[e] = mask_int[e].astype(F32).astype(BF16)
            return carry

        lax.fori_loop(i * quarter, (i + 1) * quarter, halve, 0, unroll=2)
    for copy in sent:
        copy.wait_recv()
    table[blocks:, :width, :] = incoming[...]

    def forward(q, running):
        product = lax.dot_general(
            table[plan[1, q]],
            mask_half[plan[0, q]],
            (((1,), (1,)), ((), ())),
            preferred_element_type=F32,
        )
        running = running * plan[2, q].astype(F32) + product
        sums[q] = running
        return running

    lax.fori_loop(0, edges, forward, jnp.zeros((width + ONES, block), F32), unroll=16)

    def aggregate(s):
        def one(i, carry):
            b = s * per_sub + i
            total = sums[plan[3, b]] * plan[4, b].astype(F32)
            scale = lax.rsqrt(1.0 + total[width : width + 1])
            scales[b] = jnp.broadcast_to(scale, (8, block))
            own = table[b, :width, :].astype(F32)
            agg[s, :, tile(i)] = ((own + total[:width]) * scale).astype(BF16)
            return carry

        lax.fori_loop(0, per_sub, one, 0)

    own_rows = pl.ds(pl.multiple_of(sub * width, width), width)
    across = []
    for index, s in in_sub:
        aggregate(s)
        across.append(push(agg.at[s], full.at[own_rows], a2a_sem, index, dom, s))
    aggregate(sub)
    full[own_rows, :] = agg[sub]
    w_in.wait()
    strip = features // 4
    for i in range(4):
        wt[:, i * strip : (i + 1) * strip] = w[i * strip : (i + 1) * strip, :].T
    cot_in.wait()
    for copy in across:
        copy.wait_recv()

    def half_rows(i):
        return pl.ds(pl.multiple_of(i * half, half), half)

    def transform(i):
        rows = half_rows(i)
        pre = jnp.dot(w[rows, :], full[...], preferred_element_type=F32)
        gate = 1.0 / (1.0 + jnp.exp(-pre))
        hid[rows, :] = (pre * gate).astype(BF16)
        d_pre[rows, :] = (
            cot_v[rows, :].astype(F32) * gate * (1.0 + pre * (1.0 - gate))
        ).astype(BF16)

    def term(i):
        return lax.dot_general(
            d_pre[half_rows(i), :],
            full[...],
            (((1,), (1,)), ((), ())),
            preferred_element_type=F32,
        )

    transform(1 - core)
    dw_out[...] = term(1 - core).astype(BF16)
    to_core = push(dw_out, core_in, core_sem, 0, dom, sibling)
    transform(core)
    hid_out = fetch(hid, hidden, 7)
    dw_own[...] = term(core)

    def x_rows(i):
        return pl.ds(pl.multiple_of(i * xrows, xrows), xrows)

    def gradient(i, carry):
        rows = half_rows(i)
        product = jnp.dot(wt[rows, :], d_pre[...], preferred_element_type=F32).astype(BF16)
        for k in range(per_sub):
            d_agg[k, rows, :] = product[:, k * block : (k + 1) * block]
        return carry

    lax.fori_loop(0, CORES, gradient, 0)

    to_core.wait_recv()

    def add_core(i):
        total = dw_own[x_rows(i), :] + core_in[x_rows(i), :].astype(F32)
        dw_own[x_rows(i), :] = total
        x_out[x_rows(i), :] = total.astype(BF16)

    to_x = []
    for o, other in in_x:
        add_core(other)
        to_x.append(
            push(x_out.at[x_rows(other)], x_in.at[o - 1], x_sem, o, dom, other * CORES + core)
        )
    add_core(x)


    own_blocks = pl.ds(sub * per_sub, per_sub)
    backward = [
        push(
            d_agg.at[:, pl.ds(pl.multiple_of(s * width, width), width)],
            back.at[own_blocks],
            back_sem,
            index,
            dom,
            s,
        )
        for index, s in in_sub
    ]
    back[own_blocks] = d_agg[:, own_rows, :]

    def z_part(i):
        return (
            pl.ds(pl.multiple_of((i // 2) * 16, 16), 16),
            pl.ds(pl.multiple_of((i % 2) * wide, wide), wide),
        )

    for copy in to_x:
        copy.wait_recv()
    total = dw_own[x_rows(x), :]
    for o in range(cols_x - 1):
        total = total + x_in[o].astype(F32)
    dw_own[:xrows, :] = total
    z_out[...] = total.astype(BF16)
    to_z = [
        push(z_out.at[z_part(other)], z_in.at[o - 1], z_sem, o, other * ROWS_Y + y, sub)
        for o, other in in_z
    ]
    for copy in to_z:
        copy.wait_recv()
    rows, columns = z_part(z)
    total = dw_own[rows, columns]
    for o in range(deep - 1):
        total = total + z_in[o].astype(F32)
    y_all[y] = total.astype(BF16)
    to_y = [
        push(y_all.at[y], y_all.at[y], y_sem, o, z * ROWS_Y + other, sub) for o, other in in_y
    ]
    for copy in backward:
        copy.wait_recv()

    def rescale(b, carry):
        scaled[b] = (back[b].astype(F32) * scales[b][:1]).astype(BF16)
        return carry

    lax.fori_loop(0, blocks, rescale, 0, unroll=2)

    def backward_edge(q, running):
        product = jnp.dot(scaled[plan[6, q]], mask_half[plan[5, q]], preferred_element_type=F32)
        running = running * plan[7, q].astype(F32) + product
        sums[q, :width, :] = running
        return running

    def some_edges(i, running):
        return lax.fori_loop(
            i * edges // 4, (i + 1) * edges // 4, backward_edge, running, unroll=16
        )

    running = jnp.zeros((width, block), F32)
    for part in range(1):
        running = some_edges(part, running)
    for copy in to_y:
        copy.wait_recv()
    total = y_all[0].astype(F32)
    for other in range(1, ROWS_Y):
        total = total + y_all[other].astype(F32)
    summed[...] = total.astype(BF16)

    def x_strip(of_core, of_x):
        return pl.ds(pl.multiple_of(of_core * half + of_x * xrows, xrows), xrows)

    mine = (
        pl.ds(pl.multiple_of(core * half + x * xrows + (z // 2) * 16, 16), 16),
        pl.ds(pl.multiple_of((z % 2) * wide, wide), wide),
    )
    over_z = [
        push(summed, gathered.at[mine], gz_sem, o, other * ROWS_Y + y, sub) for o, other in in_z
    ]
    gathered[mine] = summed[...]
    for part in range(1, 4):
        running = some_edges(part, running)
    home = []
    for j in reversed(range(offsets)):
        for k in range(capacity):
            t = blocks + j * capacity + k
            returning[j * capacity + k] = (
                sums[plan[8, t]][:width] * plan[9, t].astype(F32)
            ).astype(BF16)
        home.append(
            push(
                returning.at[pl.ds(j * capacity, capacity)],
                returned.at[pl.ds(j * capacity, capacity)],
                ret_sem,
                j,
                against[j],
                sub,
            )
        )
    for copy in over_z:
        copy.wait_recv()
    def to_results(of_x, index):
        rows = x_strip(core, of_x)
        own_parts.append(fetch(gathered.at[rows], d_weight.at[rows], index))
        over_core.append(
            push(gathered.at[rows], d_weight.at[rows], gc_sem, index, dom, sibling)
        )

    own_parts = []
    over_core = []
    strip_x = gathered.at[x_strip(core, x)]
    over_x = [
        push(strip_x, strip_x, gx_sem, o, dom, other * CORES + core) for o, other in in_x
    ]
    to_results(x, 0)
    def own_total(b, carry):
        base[b] = scaled[b].astype(F32) + sums[plan[8, b]][:width] * plan[9, b].astype(F32)
        return carry

    lax.fori_loop(0, blocks, own_total, 0, unroll=2)
    for copy in home:
        copy.wait_recv()

    def add_slot(i, running):
        running = running * plan[12, i].astype(F32) + returned[plan[11, i]].astype(F32)
        slot_sums[i] = running
        return running

    lax.fori_loop(0, slots, add_slot, jnp.zeros((width, block), F32))

    def finish(b, carry):
        result[:, tile(b)] = (
            base[b]
            + slot_sums[plan[13, b]] * plan[14, b].astype(F32)
        ).astype(BF16)
        return carry

    lax.fori_loop(0, blocks, finish, 0, unroll=2)
    d_feats_out = fetch(result, d_feats, 8)
    for (o, _), copy in zip(in_x, over_x):
        copy.wait_recv()
        to_results(lax.rem(x - o + cols_x, cols_x), o)
    for copy in over_core:
        copy.wait_recv()
    for copy in (
        sent
        + across
        + [to_core]
        + to_x
        + backward
        + to_z
        + to_y
        + home
        + over_z
        + over_x
        + over_core
    ):
        copy.wait_send()
    hid_out.wait()
    d_feats_out.wait()
    for copy in own_parts:
        copy.wait()


def write_kernel(
    hid, d_feats, d_weight, hid_out, d_feats_out, d_weight_out, hid_v, d_feats_v, narrow, wide, sem
):
    parts, rows, _ = narrow.shape
    columns = d_feats_v.shape[2]
    out_of = []
    into = []
    for i in range(parts):
        span, lanes = pl.ds(i * rows, rows), pl.ds(i * columns, columns)
        steps = (
            (d_weight.at[span], narrow.at[i], wide.at[i], d_weight_out.at[span]),
            (hid.at[span], hid_v.at[i], hid_v.at[i], hid_out.at[span]),
            (d_feats.at[:, lanes], d_feats_v.at[i], d_feats_v.at[i], d_feats_out.at[:, lanes]),
        )
        for j, (here, arrive, leave, there) in enumerate(steps):
            into.append(pltpu.make_async_copy(here, arrive, sem.at[0, 3 * i + j]))
            out_of.append(pltpu.make_async_copy(leave, there, sem.at[1, 3 * i + j]))
    for copy in into:
        copy.start()
    for i in range(parts):
        for j in range(3):
            into[3 * i + j].wait()
            if j == 0:
                wide[i] = narrow[i].astype(F32)
            out_of[3 * i + j].start()
    for copy in out_of:
        copy.wait()


def shards(cols_x, feats, weight, edge_dst, edge_src, edge_mask, send_list, send_count, cotangent):
    width, span = feats.shape
    _, edges, block, _ = edge_mask.shape
    features = weight.shape[0]
    blocks = span // block
    _, offsets, capacity = send_list.shape
    slots = offsets * capacity
    table_len = blocks + slots
    subs = cols_x * CORES
    labels = span // subs
    half = features // CORES
    xrows = half // cols_x
    deep = lax.axis_size("dom") // ROWS_Y
    vmem, smem, hbm, anywhere = (
        pl.BlockSpec(memory_space=space) for space in (pltpu.VMEM, pltpu.SMEM, pltpu.HBM, pl.ANY)
    )
    plan = pl.pallas_call(
        functools.partial(plan_kernel, blocks, table_len),
        out_shape=jax.ShapeDtypeStruct((16, 128), jnp.int32),
        in_specs=[smem, smem, vmem, vmem],
        out_specs=vmem,
        compiler_params=pltpu.CompilerParams(vmem_limit_bytes=VMEM_BYTES),
    )(send_list, send_count, edge_dst, edge_src)
    dma = pltpu.SemaphoreType.DMA
    hidden, d_feats, d_weight = pl.pallas_call(
        functools.partial(kernel, cols_x),
        out_shape=(
            jax.ShapeDtypeStruct((features, labels), BF16),
            jax.ShapeDtypeStruct((width, span), BF16),
            jax.ShapeDtypeStruct((features, features), BF16),
        ),
        in_specs=[smem] + [hbm] * 4,
        out_specs=(anywhere,) * 3,
        scratch_shapes=[
            pltpu.VMEM((table_len, width + ONES, block), BF16),
            pltpu.VMEM((edges, block, block), jnp.int32),
            pltpu.VMEM((edges, block, block), BF16),
            pltpu.VMEM((edges, width + ONES, block), F32),
            pltpu.VMEM((features, features), BF16),
            pltpu.VMEM((features, features), BF16),
            pltpu.VMEM((features, labels), BF16),
            pltpu.VMEM((slots, width, block), BF16),
            pltpu.VMEM((slots, width, block), BF16),
            pltpu.VMEM((subs, width, labels), BF16),
            pltpu.VMEM((features, labels), BF16),
            pltpu.VMEM((blocks, 8, block), F32),
            pltpu.VMEM((features, labels), BF16),
            pltpu.VMEM((features, labels), BF16),
            pltpu.VMEM((labels // block, features, block), BF16),
            pltpu.VMEM((half, features), BF16),
            pltpu.VMEM((half, features), F32),
            pltpu.VMEM((half, features), BF16),
            pltpu.VMEM((half, features), BF16),
            pltpu.VMEM((cols_x - 1, xrows, features), BF16),
            pltpu.VMEM((xrows, features), BF16),
            pltpu.VMEM((deep - 1, 16, features // 2), BF16),
            pltpu.VMEM((ROWS_Y, 16, features // 2), BF16),
            pltpu.VMEM((16, features // 2), BF16),
            pltpu.VMEM((features, features), BF16),
            pltpu.VMEM((blocks, width, block), BF16),
            pltpu.VMEM((blocks, width, block), BF16),
            pltpu.VMEM((slots, width, block), BF16),
            pltpu.VMEM((slots, width, block), BF16),
            pltpu.VMEM((slots, width, block), F32),
            pltpu.VMEM((blocks, width, block), F32),
            pltpu.VMEM((width, span), BF16),
            dma((10,)),
            dma((blocks,)),
            dma((2, offsets)),
            dma((2, offsets)),
            dma((2, subs)),
            dma((2, subs)),
            dma((2, 1)),
            dma((2, cols_x)),
            dma((2, deep)),
            dma((2, ROWS_Y)),
            dma((2, deep)),
            dma((2, cols_x)),
            dma((2, cols_x)),
        ],
        compiler_params=pltpu.CompilerParams(
            collective_id=0, has_side_effects=True, vmem_limit_bytes=VMEM_BYTES
        ),
    )(plan, feats, weight, edge_mask[0], cotangent)
    return pl.pallas_call(
        write_kernel,
        out_shape=(
            jax.ShapeDtypeStruct((features, labels), BF16),
            jax.ShapeDtypeStruct((width, span), BF16),
            jax.ShapeDtypeStruct((features, features), F32),
        ),
        in_specs=[anywhere] * 3,
        out_specs=(hbm,) * 3,
        scratch_shapes=[
            pltpu.VMEM((4, features // 4, labels), BF16),
            pltpu.VMEM((4, width, span // 4), BF16),
            pltpu.VMEM((4, features // 4, features), BF16),
            pltpu.VMEM((4, features // 4, features), F32),
            dma((2, 12)),
        ],
        compiler_params=pltpu.CompilerParams(vmem_limit_bytes=VMEM_BYTES),
    )(hidden, d_feats, d_weight)


def solution(mesh):
    cols_x = mesh.shape["sub"] // CORES
    return jax.shard_map(
        functools.partial(shards, cols_x),
        mesh=mesh,
        in_specs=(
            P("sub", "dom"),
            P(),
            P("dom", None),
            P("dom", None),
            P("dom", None, None, None),
            P("dom", None, None),
            P("dom", None),
            P(None, ("dom", "sub")),
        ),
        out_specs=(P(None, ("dom", "sub")), P("sub", "dom"), P()),
        check_vma=False,
    )
```
